32 devices in a mesh: groups: 2 (over y), mz: 4 (over z), pix: 4 (over x, core).
Axes of the slice: x: 2, y: 2, z: 4, core: 2. Of those that a mesh axis runs over, the one named last changes fastest.
Arguments:
- spectra: bfloat16 [1024, 262144], P(('groups', 'pix'), 'mz'), parts along dimension 0
- kernel: bfloat16 [129], replicated, may hold values from 0.0009994507 to 0.029907227
- probes: bfloat16 [262144, 128], P('mz'), may hold values from -0.01171875 to 0.01171875
Outputs:
- basis: bfloat16 [1024, 128], P(('groups', 'pix')), parts along dimension 0
- projected: bfloat16 [256, 262144], P(('groups', 'pix'), 'mz'), parts along dimension 0
The draws below stay inside these ranges and needn't reach their ends.
There are 2 independent parts, one for each index of `groups`. The reference program is written for one: setup_inputs(seed, part) draws one part's arguments, and reference() takes and returns one part's arrays. A program takes and returns all parts, laid end to end along the dimension named above; an argument that names none is the same for every part. Nothing has to cross between parts.
All inputs are finite; a program needn't handle non-finite values.
Results may differ from the reference program's by a relative error of at most 0.019.
Values may be sent and summed in bfloat16 or wider, within the bound.
No kernel may reach another device: no remote copies, remote signals or barrier semaphores. Data moves between devices by JAX's collectives and lax.ppermute only.
A program may use at most 192 MiB of HBM per device.

```python
import math
import jax
import jax.numpy as jnp
from jax import lax

BINS = 262144
PROBES = 128
BAND = 129
PIX_DEV = 128
PIXELS = 512
N_PIX = 4


def draw_spectra(key, part):
    first, second = jax.random.split(key, 2)
    phase = jax.random.uniform(second, (PIXELS, 1), jnp.float32) * 6.283
    position = jnp.arange(BINS, dtype=jnp.float32)[None, :]
    smooth = 1.5 + jnp.sin(position * (6.283 / 4096.0) + phase)
    rough = jax.random.normal(first, (PIXELS, BINS), jnp.float32)
    values = rough + smooth
    return values.astype(jnp.bfloat16)


def steps_of(rng, dims, cuts, low, high):
    def one(dim, shards_of):
        heights = jax.random.uniform(jax.random.fold_in(jax.random.fold_in(rng, 6), dim), (shards_of,), jnp.float32, low / len(cuts), high / len(cuts))
        return jnp.repeat(jnp.exp(heights), dims[dim] // shards_of).reshape((-1,) + (1,) * (len(dims) - dim - 1))

    factor_of = one(*cuts[0])
    for cut in cuts[1:]:
        factor_of = factor_of * one(*cut)
    return factor_of


def noise(stream_key, dims, width, bound, pieces=(), kind=jnp.bfloat16):
    values = width * jax.random.normal(stream_key, dims, jnp.float32)
    if pieces:
        values = values * steps_of(stream_key, dims, pieces, -0.22, 0.18)
    return jnp.clip(values, -bound, bound).astype(kind)


def setup_inputs(seed: int = 0, part: int = 0) -> dict:
    key_of = jax.random.split(jax.random.key(seed), 4)
    own_keys = jax.random.split(jax.random.fold_in(key_of[3], part), 4)
    spectra = draw_spectra(jax.random.fold_in(jax.random.fold_in(key_of[3], part), 71), part)
    kernel = jnp.clip(jnp.exp(jax.random.uniform(key_of[1], (BAND,), jnp.float32, math.log(0.0009994507), math.log(0.029907227))), 0.0009994507, 0.029907227).astype(jnp.bfloat16)
    probes = noise(key_of[2], (BINS, PROBES), BINS ** -0.5, 0.01171875, ((0, 4),))
    return {"spectra": spectra, "kernel": kernel, "probes": probes}


def smooth_block(rows, kernel):
    lhs = rows.astype(jnp.float32)[:, None, :]
    rhs = kernel.astype(jnp.float32)[None, None, :]
    base = lax.conv_general_dilated(lhs, rhs, (1,), ((64, 64),), dimension_numbers=('NCH', 'OIH', 'NCH'), precision=lax.Precision.HIGHEST)[:, 0, :]
    return (rows.astype(jnp.float32) - base).astype(jnp.bfloat16)

def reference(spectra, kernel, probes):
    blocks = spectra.reshape(N_PIX, PIX_DEV, BINS)
    cleaned_blocks = lax.map(lambda rows: smooth_block(rows, kernel), blocks)
    cleaned = cleaned_blocks.reshape(PIXELS, BINS)
    sketch = jnp.dot(cleaned.astype(jnp.float32), probes.astype(jnp.float32), preferred_element_type=jnp.float32)
    gram = jnp.dot(sketch.T, sketch, precision=lax.Precision.HIGHEST) / float(PIXELS)
    lower = jnp.linalg.cholesky(gram)
    basis_f = lax.linalg.triangular_solve(lower, sketch, left_side=False, lower=True, transpose_a=True)
    basis = basis_f.astype(jnp.bfloat16)
    factor = 1.0 / math.sqrt(float(PIXELS))
    total = jnp.zeros((PROBES, BINS), jnp.float32)
    for index in range(N_PIX):
        rows = basis[index * PIX_DEV:(index + 1) * PIX_DEV]
        part_sum = jnp.dot(rows.T.astype(jnp.float32), cleaned_blocks[index].astype(jnp.float32), preferred_element_type=jnp.float32) * factor
        total = total + part_sum.astype(jnp.bfloat16).astype(jnp.float32)
    return (basis, total.astype(jnp.bfloat16))
```

```python
import functools
import math

import jax
import jax.numpy as jnp
from jax import lax
from jax.experimental import pallas as pl
from jax.experimental.pallas import tpu as pltpu
from jax.sharding import PartitionSpec as P

F32 = jnp.float32
BF16 = jnp.bfloat16
HIGHEST = lax.Precision.HIGHEST
TILE = 128
WIDTH = 256
REACH = 64
VMEM = pl.BlockSpec(memory_space=pltpu.VMEM)


def params(limit=56):
    return pltpu.CompilerParams(vmem_limit_bytes=limit * 2**20)


def partner(x, axis, shift):
    count = lax.axis_size(axis)
    return lax.ppermute(x, axis, [(i, i ^ shift) for i in range(count)])


def spread(x, axis):
    count = lax.axis_size(axis)
    if count & (count - 1):
        return [lax.psum(x, axis)]
    shift = count // 2
    while shift >= 4:
        x = x + partner(x, axis, shift)
        shift //= 2
    return [x] + [partner(x, axis, s) for s in range(1, min(count, 4))]


def pairwise(parts):
    while len(parts) > 1:
        parts = [a + b for a, b in zip(parts[::2], parts[1::2])]
    return parts[0]


def band_of(taps):
    wide = jnp.broadcast_to(taps, (WIDTH, 2 * WIDTH))
    return pltpu.roll(wide, 0, 1, stride=1, stride_axis=0).T.astype(BF16)


def clean(before, block, after, band):
    ext = jnp.concatenate([before, block, after], axis=1)
    rows, bins = block.shape
    starts = range(0, bins, WIDTH)
    lhs = jnp.concatenate([ext[:, a : a + 2 * WIDTH] for a in starts], axis=0)
    base = jnp.dot(lhs, band, preferred_element_type=F32)
    mid = jnp.concatenate([block[:, a : a + WIDTH] for a in starts], axis=0)
    out = (mid.astype(F32) - base).astype(BF16)
    return jnp.concatenate([out[i * rows : (i + 1) * rows] for i in range(bins // WIDTH)], axis=1)


def sketch_kernel(steps, taps, block, prev, after, low, high, probes, sketch, band):
    i = pl.program_id(0)

    @pl.when(i == 0)
    def _():
        band[...] = band_of(taps[...])
        sketch[...] = jnp.zeros_like(sketch)

    cleaned = clean(
        jnp.where(i == 0, low[...], prev[...]),
        block[...],
        jnp.where(i == steps - 1, high[...], after[...]),
        band[...],
    )
    sketch[...] += jnp.dot(cleaned, probes[...], preferred_element_type=F32)


ANY = pl.BlockSpec(memory_space=pl.ANY)


def whole(shape):
    return pl.BlockSpec(shape, lambda i: (0, 0))


def block_specs(rows, size, first, last):
    per = size // TILE
    return [
        pl.BlockSpec((rows, size), lambda i: (0, first + i)),
        pl.BlockSpec((rows, TILE), lambda i: (0, jnp.maximum((first + i) * per - 1, 0))),
        pl.BlockSpec((rows, TILE), lambda i: (0, jnp.minimum((first + i + 1) * per, last))),
    ]


def sketch_of(taps, spectra, low, high, probes):
    rows, bins = spectra.shape
    size = math.gcd(bins, 8192)
    steps = bins // size
    columns = probes.shape[1]
    return pl.pallas_call(
        functools.partial(sketch_kernel, steps),
        grid=(steps,),
        in_specs=[whole(taps.shape)]
        + block_specs(rows, size, 0, bins // TILE - 1)
        + [whole(low.shape), whole(high.shape)]
        + [pl.BlockSpec((size, columns), lambda i: (i, 0))],
        out_specs=[whole((rows, columns)), whole((2 * WIDTH, WIDTH))],
        out_shape=[
            jax.ShapeDtypeStruct((rows, columns), F32),
            jax.ShapeDtypeStruct((2 * WIDTH, WIDTH), BF16),
        ],
        compiler_params=params(),
    )(taps, spectra, spectra, spectra, low, high, probes)


def gram_kernel(*refs):
    parts, sketch, gram = refs[:-2], refs[-2], refs[-1]
    total = pairwise([part[...] for part in parts])
    sketch[...] = total
    gram[...] = lax.dot_general(
        total, total, (((0,), (0,)), ((), ())), precision=HIGHEST, preferred_element_type=F32
    )


def gram_of(parts):
    shape = parts[0].shape
    return pl.pallas_call(
        gram_kernel,
        in_specs=[VMEM] * len(parts),
        out_specs=[VMEM] * 2,
        out_shape=[
            jax.ShapeDtypeStruct(shape, F32),
            jax.ShapeDtypeStruct((shape[1], shape[1]), F32),
        ],
        compiler_params=params(32),
    )(*parts)


def inverse_factor(gram):
    size = gram.shape[0]
    groups = range(size // 8)
    rows = [gram[8 * g : 8 * g + 8] for g in groups]
    lane = lax.broadcasted_iota(jnp.int32, (8, size), 1)
    sub = lax.broadcasted_iota(jnp.int32, (8, size), 0)

    def row_of(x, k):
        return jnp.broadcast_to(x[k : k + 1], (8, size))

    result = []
    for g in groups:
        inside = (lane >= 8 * g) & (lane < 8 * g + 8)
        below = groups[g:]
        cols = {
            h: [
                jnp.broadcast_to(rows[h][:, 8 * g + k : 8 * g + k + 1], (8, size))
                for k in range(8)
            ]
            for h in below
        }
        for h in below:
            unit = jnp.where(lane - 8 * g == sub, 1.0, 0.0) if h == g else 0.0
            rows[h] = jnp.where(inside, unit, rows[h])
        pivots = jnp.ones((8, size), F32)
        for k in range(8):
            pivot = row_of(cols[g][k], k)
            scale = 1.0 / pivot
            pivots = jnp.where(sub == k, pivot, pivots)
            line = row_of(rows[g], k) * scale
            heads = {m: row_of(cols[g][m], k) * scale for m in range(k + 1, 8)}
            for h in below:
                c = cols[h][k]
                if h == g:
                    c = jnp.where(sub > k, c, 0.0)
                rows[h] = rows[h] - c * line
                for m in range(k + 1, 8):
                    cols[h][m] = cols[h][m] - c * heads[m]
        result.append(jnp.where(lane < 8 * g + 8, rows[g] * lax.rsqrt(pivots), 0.0))
    return jnp.concatenate(result, axis=0)


def basis_kernel(pixels, chips, *refs):
    parts, sketch, basis, turned = refs[:-3], refs[-3], refs[-2], refs[-1]
    gram = pairwise([part[...] for part in parts]) / float(pixels)
    inverse = inverse_factor(gram)
    size = gram.shape[0]
    across = lax.dot_general(
        inverse, sketch[...], (((1,), (1,)), ((), ())), precision=HIGHEST,
        preferred_element_type=F32,
    )
    basis[...] = across.T.astype(BF16)
    share = size // (2 * chips)
    me = lax.axis_index("pix")
    to = lax.broadcasted_iota(jnp.int32, (size, size), 0)
    source = lax.broadcasted_iota(jnp.int32, (size, size), 1)
    block = to // share
    other = block // chips
    chip = lax.rem(lax.rem(block, chips) + me // 2, chips)
    core = jnp.where(other == 1, 1 - lax.rem(me, 2), lax.rem(me, 2))
    wanted = (2 * chip + core) * share + lax.rem(to, share)
    pick = jnp.where(wanted == source, 1.0, 0.0).astype(BF16)
    turned[...] = jnp.dot(pick, across.astype(BF16), preferred_element_type=F32).astype(BF16)


def basis_of(parts, sketch, pixels, chips):
    rows, size = sketch.shape
    return pl.pallas_call(
        functools.partial(basis_kernel, pixels, chips),
        in_specs=[VMEM] * (len(parts) + 1),
        out_specs=[VMEM] * 2,
        out_shape=[
            jax.ShapeDtypeStruct((rows, size), BF16),
            jax.ShapeDtypeStruct((size, rows), BF16),
        ],
        compiler_params=params(32),
    )(*parts, sketch)


def project_kernel(first, last, factor, *refs):
    turned, band, block, prev, after, low, high = refs[:7]
    keep, give = refs[-2:]
    i = first + pl.program_id(0)
    cleaned = clean(
        jnp.where(i == 0, low[...], prev[...]),
        block[...],
        jnp.where(i == last, high[...], after[...]),
        band[...],
    )
    part = jnp.dot(turned[...], cleaned, preferred_element_type=F32) * factor
    half = keep.shape[0]
    keep[...] = part[:half].astype(BF16)
    give[...] = part[half:].astype(BF16)


def project(turned, band, spectra, low, high, start, count, factor, wait):
    rows, bins = spectra.shape
    size = math.gcd(math.gcd(start, count), 4096)
    first = start // size
    half = turned.shape[0] // 2
    out = pl.BlockSpec((half, size), lambda i: (0, i))
    shape = jax.ShapeDtypeStruct((half, count), BF16)
    return pl.pallas_call(
        functools.partial(project_kernel, first, bins // size - 1, factor),
        grid=(count // size,),
        in_specs=[whole(turned.shape), whole(band.shape)]
        + block_specs(rows, size, first, bins // TILE - 1)
        + [whole(low.shape), whole(high.shape)]
        + [ANY] * len(wait),
        out_specs=[out, out],
        out_shape=[shape, shape],
        compiler_params=params(50),
    )(turned, band, spectra, spectra, spectra, low, high, *wait)


def merge_kernel(share, chips, keep, got, *refs):
    outs = refs[-chips:]
    total = (keep[...].astype(F32) + got[...].astype(F32)).astype(BF16)
    for k, out in enumerate(outs):
        out[...] = total[k * share : (k + 1) * share]


def merge(keep, got, chips, wait):
    half, count = keep.shape
    share = half // chips
    size = math.gcd(count, 8192)
    return pl.pallas_call(
        functools.partial(merge_kernel, share, chips),
        grid=(count // size,),
        in_specs=[pl.BlockSpec((half, size), lambda i: (0, i))] * 2 + [ANY] * len(wait),
        out_specs=[pl.BlockSpec((share, size), lambda i: (0, i))] * chips,
        out_shape=[jax.ShapeDtypeStruct((share, count), BF16)] * chips,
        compiler_params=params(32),
    )(keep, got, *wait)


def finish_kernel(count, *refs):
    parts, out, done = refs[:count], refs[-2], refs[-1]
    done[...] = jnp.zeros_like(done)
    total = parts[0][...].astype(F32)
    for part in parts[1:]:
        total = total + part[...].astype(F32)
    out[...] = total.astype(BF16)


def finish(out, parts, start, bins, wait):
    share, count = parts[0].shape
    size = math.gcd(math.gcd(count, start), 8192)
    first = start // size
    place = pl.BlockSpec((share, size), lambda i: (0, first + i))
    extra = [] if out is None else [out]
    return pl.pallas_call(
        functools.partial(finish_kernel, len(parts)),
        grid=(count // size,),
        in_specs=[pl.BlockSpec((share, size), lambda i: (0, i))] * len(parts)
        + [ANY] * (len(extra) + len(wait)),
        out_specs=[place, whole((8, TILE))],
        out_shape=[
            jax.ShapeDtypeStruct((share, bins), BF16),
            jax.ShapeDtypeStruct((8, TILE), F32),
        ],
        input_output_aliases={len(parts): 0} if extra else {},
        compiler_params=params(32),
    )(*parts, *extra, *wait)


def chunks_of(bins):
    sizes = []
    left = bins
    for size in (2048, 6144):
        if left > size:
            sizes.append(size)
            left -= size
    while left > 0:
        size = min(8192, left)
        sizes.append(size)
        left -= size
    return sizes


def per_device(spectra, kernel, probes):
    rows, bins = spectra.shape
    pix = lax.axis_size("pix")
    depth = lax.axis_size("mz")
    chips = pix // 2
    pixels = rows * pix
    factor = 1.0 / math.sqrt(float(pixels))

    up = [(i, i + 1) for i in range(depth - 1)]
    down = [(i + 1, i) for i in range(depth - 1)]
    low = lax.ppermute(spectra[:, bins - TILE :], "mz", up)
    high = lax.ppermute(spectra[:, :TILE], "mz", down)
    taps = jnp.pad(kernel.astype(F32), (REACH, 2 * WIDTH - REACH - kernel.shape[0]))[None]

    partial_sketch, band = sketch_of(taps, spectra, low, high, probes)
    sketch, partial_gram = gram_of(spread(partial_sketch, "mz"))
    basis, turned = basis_of(spread(partial_gram, "pix"), sketch, pixels, chips)

    counts = chunks_of(bins)
    starts = [sum(counts[:k]) for k in range(len(counts))]
    routes = [
        [
            (2 * chip + core, 2 * ((chip + k) % chips) + core)
            for chip in range(chips)
            for core in range(2)
        ]
        for k in range(chips)
    ]

    def project_at(k, wait):
        return project(turned, band, spectra, low, high, starts[k], counts[k], factor, wait)

    out, sent = None, []
    ready = project_at(0, [])
    for k in range(len(counts)):
        keep, give = ready
        got = partner(give, "pix", 1)
        recent = [give]
        if k + 1 < len(counts):
            ready = project_at(k + 1, recent + [parts[0] for parts in sent[-1:]])
            recent = [ready[1]]
        if k >= 2:
            out, done = finish(out, sent[k - 2], starts[k - 2], bins, recent)
            recent = [done]
        mine = merge(keep, got, chips, recent)
        sent.append(
            [mine[0]] + [lax.ppermute(mine[m], "pix", routes[m]) for m in range(1, chips)]
        )
    for k in range(max(len(counts) - 2, 0), len(counts)):
        out, done = finish(out, sent[k], starts[k], bins, [])
    return (basis, out)


def solution(mesh):
    in_specs = (P(("groups", "pix"), "mz"), P(), P("mz", None))
    out_specs = (P(("groups", "pix"), None), P(("groups", "pix"), "mz"))
    return jax.shard_map(
        per_device, mesh=mesh, in_specs=in_specs, out_specs=out_specs, check_vma=False
    )
```

```python
import functools
import math

import jax
import jax.numpy as jnp
from jax import lax
from jax.experimental import pallas as pl
from jax.experimental.pallas import tpu as pltpu
from jax.sharding import PartitionSpec as P

F32 = jnp.float32
BF16 = jnp.bfloat16
HIGHEST = lax.Precision.HIGHEST
TILE = 128
WIDTH = 256
REACH = 64
CHUNK = 8192
VMEM = pl.BlockSpec(memory_space=pltpu.VMEM)


COST = pl.CostEstimate(flops=1, bytes_accessed=1, transcendentals=0)


def params(limit=56):
    return pltpu.CompilerParams(vmem_limit_bytes=limit * 2**20)


def partner(x, axis, shift):
    count = lax.axis_size(axis)
    return lax.ppermute(x, axis, [(i, i ^ shift) for i in range(count)])


def gather(x, axis):
    count = lax.axis_size(axis)
    if count & (count - 1):
        every = lax.all_gather(x, axis)
        return [every[k] for k in range(count)]
    return [x] + [partner(x, axis, shift) for shift in range(1, count)]


def spread(x, axis):
    count = lax.axis_size(axis)
    if count & (count - 1):
        return [lax.psum(x, axis)]
    shift = count // 2
    while shift >= 4:
        x = x + partner(x, axis, shift)
        shift //= 2
    return [x] + [partner(x, axis, s) for s in range(1, min(count, 4))]


def pairwise(parts):
    while len(parts) > 1:
        odd = [parts[-1]] if len(parts) % 2 else []
        parts = [a + b for a, b in zip(parts[::2], parts[1::2])] + odd
    return parts[0]


def band_of(taps):
    wide = jnp.broadcast_to(taps, (WIDTH, 2 * WIDTH))
    return pltpu.roll(wide, 0, 1, stride=1, stride_axis=0).T.astype(BF16)


def clean(before, block, after, band):
    ext = jnp.concatenate([before, block, after], axis=1)
    rows, bins = block.shape
    starts = range(0, bins, WIDTH)
    lhs = jnp.concatenate([ext[:, a : a + 2 * WIDTH] for a in starts], axis=0)
    base = jnp.dot(lhs, band, preferred_element_type=F32)
    mid = jnp.concatenate([block[:, a : a + WIDTH] for a in starts], axis=0)
    out = (mid.astype(F32) - base).astype(BF16)
    return jnp.concatenate([out[i * rows : (i + 1) * rows] for i in range(bins // WIDTH)], axis=1)


def sketch_kernel(steps, taps, block, prev, after, low, high, probes, sketch, band, edges):
    i = pl.program_id(0)

    @pl.when(i == 0)
    def _():
        band[...] = band_of(taps[...])
        sketch[...] = jnp.zeros_like(sketch)

    cleaned = clean(
        jnp.where(i == 0, low[...], prev[...]),
        block[...],
        jnp.where(i == steps - 1, high[...], after[...]),
        band[...],
    )
    sketch[...] += jnp.dot(cleaned, probes[...], preferred_element_type=F32)

    @pl.when((i == 0) | (i == steps - 1))
    def _():
        edges[...] = cleaned


ANY = pl.BlockSpec(memory_space=pl.ANY)


def whole(shape):
    return pl.BlockSpec(shape, lambda i: (0, 0))


def block_specs(rows, size, first, last):
    per = size // TILE
    return [
        pl.BlockSpec((rows, size), lambda i: (0, first + i)),
        pl.BlockSpec((rows, TILE), lambda i: (0, jnp.maximum((first + i) * per - 1, 0))),
        pl.BlockSpec((rows, TILE), lambda i: (0, jnp.minimum((first + i + 1) * per, last))),
    ]


def sketch_of(taps, spectra, low, high, probes, size):
    rows, bins = spectra.shape
    steps = bins // size
    columns = probes.shape[1]
    return pl.pallas_call(
        functools.partial(sketch_kernel, steps),
        grid=(steps,),
        in_specs=[whole(taps.shape)]
        + block_specs(rows, size, 0, bins // TILE - 1)
        + [whole(low.shape), whole(high.shape)]
        + [pl.BlockSpec((size, columns), lambda i: (i, 0))],
        out_specs=[
            whole((rows, columns)),
            whole((2 * WIDTH, WIDTH)),
            pl.BlockSpec((rows, size), lambda i: (0, (i + 1) // steps)),
        ],
        out_shape=[
            jax.ShapeDtypeStruct((rows, columns), F32),
            jax.ShapeDtypeStruct((2 * WIDTH, WIDTH), BF16),
            jax.ShapeDtypeStruct((rows, 2 * size), BF16),
        ],
        cost_estimate=COST,
        compiler_params=params(48),
    )(taps, spectra, spectra, spectra, low, high, probes)


def total_kernel(*refs):
    refs[-1][...] = pairwise([part[...] for part in refs[:-1]])


def total_of(parts):
    return pl.pallas_call(
        total_kernel,
        in_specs=[VMEM] * len(parts),
        out_specs=VMEM,
        out_shape=jax.ShapeDtypeStruct(parts[0].shape, F32),
        cost_estimate=COST,
        compiler_params=params(32),
    )(*parts)


def inverse_factor(gram):
    size = gram.shape[0]
    groups = range(size // 8)
    rows = [gram[8 * g : 8 * g + 8] for g in groups]
    lane = lax.broadcasted_iota(jnp.int32, (8, size), 1)
    sub = lax.broadcasted_iota(jnp.int32, (8, size), 0)

    def row_of(x, k):
        return jnp.broadcast_to(x[k : k + 1], (8, size))

    result = []
    for g in groups:
        inside = (lane >= 8 * g) & (lane < 8 * g + 8)
        below = groups[g:]
        cols = {
            h: [
                jnp.broadcast_to(rows[h][:, 8 * g + k : 8 * g + k + 1], (8, size))
                for k in range(8)
            ]
            for h in below
        }
        for h in below:
            unit = jnp.where(lane - 8 * g == sub, 1.0, 0.0) if h == g else 0.0
            rows[h] = jnp.where(inside, unit, rows[h])
        pivots = jnp.ones((8, size), F32)
        for k in range(8):
            pivot = row_of(cols[g][k], k)
            scale = 1.0 / pivot
            pivots = jnp.where(sub == k, pivot, pivots)
            line = row_of(rows[g], k) * scale
            heads = {m: row_of(cols[g][m], k) * scale for m in range(k + 1, 8)}
            for h in below:
                c = cols[h][k]
                if h == g:
                    c = jnp.where(sub > k, c, 0.0)
                rows[h] = rows[h] - c * line
                for m in range(k + 1, 8):
                    cols[h][m] = cols[h][m] - c * heads[m]
        result.append(jnp.where(lane < 8 * g + 8, rows[g] * lax.rsqrt(pivots), 0.0))
    return jnp.concatenate(result, axis=0)


def basis_kernel(chips, *refs):
    sketches, (basis, turned) = [ref[...] for ref in refs[:-2]], refs[-2:]
    rows, size = sketches[0].shape
    grams = [
        lax.dot_general(
            one, one, (((0,), (0,)), ((), ())), precision=HIGHEST, preferred_element_type=F32
        )
        for one in sketches
    ]
    inverse = inverse_factor(pairwise(grams) / float(rows * len(sketches)))
    used = jnp.concatenate(sketches[: turned.shape[1] // rows], axis=0)
    across = lax.dot_general(
        inverse, used, (((1,), (1,)), ((), ())), precision=HIGHEST, preferred_element_type=F32
    )
    basis[...] = across[:, :rows].T.astype(BF16)
    share = size // (2 * chips)
    me = lax.axis_index("pix")
    shape = (size // 2, size)
    to = lax.broadcasted_iota(jnp.int32, shape, 0)
    source = lax.broadcasted_iota(jnp.int32, shape, 1)
    chip = lax.rem(to // share + me // 2, chips)
    wanted = (2 * chip + lax.rem(me, 2)) * share + lax.rem(to, share)
    pick = jnp.where(wanted == source, 1.0, 0.0).astype(BF16)
    turned[...] = jnp.dot(pick, across.astype(BF16), preferred_element_type=F32).astype(BF16)


def basis_of(sketches, chips, used):
    rows, size = sketches[0].shape
    return pl.pallas_call(
        functools.partial(basis_kernel, chips),
        in_specs=[VMEM] * len(sketches),
        out_specs=[VMEM] * 2,
        out_shape=[
            jax.ShapeDtypeStruct((rows, size), BF16),
            jax.ShapeDtypeStruct((size // 2, used * rows), BF16),
        ],
        cost_estimate=COST,
        compiler_params=params(32),
    )(*sketches)


def put_parts(turned, cleaned, factor, outs):
    used = cleaned.shape[0]
    part = jnp.dot(turned[:, :used], cleaned, preferred_element_type=F32) * factor
    share = outs[0].shape[0]
    for k, out in enumerate(outs):
        out[...] = part[k * share : (k + 1) * share].astype(BF16)


def project_ready_kernel(factor, chips, turned, own, near, *refs):
    outs, done = refs[-1 - chips : -1], refs[-1]
    done[...] = jnp.zeros_like(done)
    put_parts(turned, jnp.concatenate([own[...], near[...]], axis=0), factor, outs)


def project_ready(turned, own, near, start, count, factor, chips, wait):
    rows = own.shape[0]
    size = math.gcd(math.gcd(start, count), 4096)
    share = turned.shape[0] // chips
    return pl.pallas_call(
        functools.partial(project_ready_kernel, factor, chips),
        grid=(count // size,),
        in_specs=[whole(turned.shape)]
        + [pl.BlockSpec((rows, size), lambda i: (0, start // size + i))] * 2
        + [ANY] * len(wait),
        out_specs=[pl.BlockSpec((share, size), lambda i: (0, i))] * chips
        + [whole((8, TILE))],
        out_shape=[jax.ShapeDtypeStruct((share, count), BF16)] * chips
        + [jax.ShapeDtypeStruct((8, TILE), F32)],
        cost_estimate=COST,
        compiler_params=params(60),
    )(turned, own, near, *wait)


def project_kernel(factor, chips, passed, turned, band, *refs):
    blocks = refs[:6]
    outs, done = refs[len(refs) - passed - 1 - chips :][:chips], refs[-1 - passed]
    done[...] = jnp.zeros_like(done)
    put_parts(turned, clean_all(blocks, band[...]), factor, outs)


def clean_all(blocks, band):
    return jnp.concatenate(
        [
            clean(blocks[n + 1][...], blocks[n][...], blocks[n + 2][...], band)
            for n in range(0, len(blocks), 3)
        ],
        axis=0,
    )


def project(turned, band, spectra, near, start, count, factor, chips, wait, passed):
    rows, bins = spectra.shape
    size = math.gcd(math.gcd(start, count), 4096)
    share = turned.shape[0] // chips
    return pl.pallas_call(
        functools.partial(project_kernel, factor, chips, len(passed)),
        grid=(count // size,),
        in_specs=[whole(turned.shape), whole(band.shape)]
        + block_specs(rows, size, start // size, bins // TILE - 1) * 2
        + [ANY] * (len(wait) + len(passed)),
        out_specs=[pl.BlockSpec((share, size), lambda i: (0, i))] * chips
        + [whole((8, TILE))]
        + [ANY] * len(passed),
        out_shape=[jax.ShapeDtypeStruct((share, count), BF16)] * chips
        + [jax.ShapeDtypeStruct((8, TILE), F32)]
        + [jax.ShapeDtypeStruct(one.shape, one.dtype) for one in passed],
        input_output_aliases={8 + len(wait) + n: chips + 1 + n for n in range(len(passed))},
        cost_estimate=COST,
        compiler_params=params(50),
    )(turned, band, spectra, spectra, spectra, near, near, near, *wait, *passed)


def project_whole_kernel(factor, turned, band, *refs):
    blocks, out, done = refs[:12], refs[-2], refs[-1]
    done[...] = jnp.zeros_like(done)
    put_parts(turned[: out.shape[0]], clean_all(blocks, band[...]), factor, [out])


def project_whole(out, turned, band, spectra, near, far, start, factor, wait):
    rows, bins = spectra.shape
    count = far[0].shape[1] - 2 * TILE
    size = math.gcd(math.gcd(start, count), 4096)
    first = start // size
    steps, per = count // size, size // TILE
    far_specs = [
        pl.BlockSpec((rows, size), lambda i: (0, i)),
        pl.BlockSpec((rows, TILE), lambda i: (0, jnp.where(i == 0, steps * per, i * per - 1))),
        pl.BlockSpec(
            (rows, TILE),
            lambda i: (0, jnp.where(i == steps - 1, steps * per + 1, (i + 1) * per)),
        ),
    ]
    share = out.shape[0]
    return pl.pallas_call(
        functools.partial(project_whole_kernel, factor),
        grid=(steps,),
        in_specs=[whole(turned.shape), whole(band.shape)]
        + block_specs(rows, size, first, bins // TILE - 1) * 2
        + far_specs * 2
        + [ANY] * (1 + len(wait)),
        out_specs=[pl.BlockSpec((share, size), lambda i: (0, first + i)), whole((8, TILE))],
        out_shape=[
            jax.ShapeDtypeStruct(out.shape, BF16),
            jax.ShapeDtypeStruct((8, TILE), F32),
        ],
        input_output_aliases={14: 0},
        cost_estimate=COST,
        compiler_params=params(50),
    )(turned, band, *[spectra] * 3, *[near] * 3, *[far[0]] * 3, *[far[1]] * 3, out, *wait)


def finish_kernel(count, *refs):
    parts, out, done = refs[:count], refs[-2], refs[-1]
    done[...] = jnp.zeros_like(done)
    total = parts[0][...].astype(F32)
    for part in parts[1:]:
        total = total + part[...].astype(F32)
    out[...] = total.astype(BF16)


def finish(out, parts, start, bins, wait):
    share, count = parts[0].shape
    size = math.gcd(math.gcd(count, start), 8192)
    first = start // size
    place = pl.BlockSpec((share, size), lambda i: (0, first + i))
    extra = [] if out is None else [out]
    return pl.pallas_call(
        functools.partial(finish_kernel, len(parts)),
        grid=(count // size,),
        in_specs=[pl.BlockSpec((share, size), lambda i: (0, i))] * len(parts)
        + [ANY] * (len(extra) + len(wait)),
        out_specs=[place, whole((8, TILE))],
        out_shape=[
            jax.ShapeDtypeStruct((share, bins), BF16),
            jax.ShapeDtypeStruct((8, TILE), F32),
        ],
        input_output_aliases={len(parts): 0} if extra else {},
        cost_estimate=COST,
        compiler_params=params(32),
    )(*parts, *extra, *wait)


def chunks_of(bins, size, early):
    chunks = [(a, size) for a in range(0, bins, size) if a != early]
    start, _ = chunks.pop()
    return chunks + [(start, size // 2), (start + size // 2, size // 2)]


def per_device(spectra, kernel, probes):
    rows, bins = spectra.shape
    pix = lax.axis_size("pix")
    depth = lax.axis_size("mz")
    chips = pix // 2
    factor = 1.0 / math.sqrt(float(rows * pix))

    up = [(i, i + 1) for i in range(depth - 1)]
    down = [(i + 1, i) for i in range(depth - 1)]
    low = lax.ppermute(spectra[:, bins - TILE :], "mz", up)
    high = lax.ppermute(spectra[:, :TILE], "mz", down)
    taps = jnp.pad(kernel.astype(F32), (REACH, 2 * WIDTH - REACH - kernel.shape[0]))[None]

    near = partner(spectra, "pix", 1)
    size = math.gcd(bins, CHUNK)
    early = None
    far = None
    if early is not None:
        end = early + size
        far = partner(
            jnp.concatenate(
                [
                    spectra[:, early:end],
                    spectra[:, early - TILE : early],
                    spectra[:, end : end + TILE],
                ],
                axis=1,
            ),
            "pix",
            2,
        )
    partial_sketch, band, edges = sketch_of(taps, spectra, low, high, probes, size)
    near_edges = partner(edges, "pix", 1)
    sketch = total_of(spread(partial_sketch, "mz"))
    basis, turned = basis_of(gather(sketch, "pix"), chips, 2 if far is None else 4)

    routes = [
        [
            (2 * chip + core, 2 * ((chip + k) % chips) + core)
            for chip in range(chips)
            for core in range(2)
        ]
        for k in range(chips)
    ]

    out, sent, recent = None, [], []
    chunks = chunks_of(bins, size, early)
    for k, (start, count) in enumerate(chunks):
        inner = 0 < start < bins - size
        if inner:
            passed = [] if far is None or len(sent) != 1 else [far]
            *mine, done = project(
                turned, band, spectra, near, start, count, factor, chips, recent, passed
            )
            if passed:
                mine, done, far = mine[:-1], mine[-1], done
        else:
            at = start if start < size else start - bins + 2 * size
            *mine, done = project_ready(
                turned, edges, near_edges, at, count, factor, chips, recent
            )
        recent = [done]
        sent.append(
            [mine[0]] + [lax.ppermute(mine[m], "pix", routes[m]) for m in range(1, chips)]
        )
        if k == len(chunks) - 1 and far is not None:
            out, done = project_whole(
                out, turned, band, spectra, near, [far, partner(far, "pix", 1)], early, factor,
                recent,
            )
            recent = [done]
        if k >= 1:
            out, done = finish(out, sent[k - 1], chunks[k - 1][0], bins, recent)
            recent = [done]
    out, done = finish(out, sent[-1], chunks[-1][0], bins, recent)
    return (basis, out)


def solution(mesh):
    in_specs = (P(("groups", "pix"), "mz"), P(), P("mz", None))
    out_specs = (P(("groups", "pix"), None), P(("groups", "pix"), "mz"))
    return jax.shard_map(
        per_device, mesh=mesh, in_specs=in_specs, out_specs=out_specs, check_vma=False
    )
```

```python
import functools
import math

import jax
import jax.numpy as jnp
from jax import lax
from jax.experimental import pallas as pl
from jax.experimental.pallas import tpu as pltpu
from jax.sharding import PartitionSpec as P

F32 = jnp.float32
BF16 = jnp.bfloat16
HIGHEST = lax.Precision.HIGHEST
TILE = 128
WIDTH = 256
REACH = 64
EDGE = 4096
VMEM = pl.BlockSpec(memory_space=pltpu.VMEM)


COST = pl.CostEstimate(flops=1, bytes_accessed=1, transcendentals=0)


def params(limit=56):
    return pltpu.CompilerParams(vmem_limit_bytes=limit * 2**20)


def partner(x, axis, shift):
    count = lax.axis_size(axis)
    return lax.ppermute(x, axis, [(i, i ^ shift) for i in range(count)])


def gather(x, axis):
    count = lax.axis_size(axis)
    if count & (count - 1):
        every = lax.all_gather(x, axis)
        return [every[k] for k in range(count)]
    return [x] + [partner(x, axis, shift) for shift in range(1, count)]


def spread(x, axis):
    count = lax.axis_size(axis)
    if count & (count - 1):
        return [lax.psum(x, axis)]
    shift = count // 2
    while shift >= 4:
        x = x + partner(x, axis, shift)
        shift //= 2
    return [x] + [partner(x, axis, s) for s in range(1, min(count, 4))]


def pairwise(parts):
    while len(parts) > 1:
        odd = [parts[-1]] if len(parts) % 2 else []
        parts = [a + b for a, b in zip(parts[::2], parts[1::2])] + odd
    return parts[0]


def band_of(taps):
    wide = jnp.broadcast_to(taps, (WIDTH, 2 * WIDTH))
    return pltpu.roll(wide, 0, 1, stride=1, stride_axis=0).T.astype(BF16)


def clean(before, block, after, band):
    ext = jnp.concatenate([before, block, after], axis=1)
    rows, bins = block.shape
    starts = range(0, bins, WIDTH)
    lhs = jnp.concatenate([ext[:, a : a + 2 * WIDTH] for a in starts], axis=0)
    base = jnp.dot(lhs, band, preferred_element_type=F32)
    mid = jnp.concatenate([block[:, a : a + WIDTH] for a in starts], axis=0)
    out = (mid.astype(F32) - base).astype(BF16)
    return jnp.concatenate([out[i * rows : (i + 1) * rows] for i in range(bins // WIDTH)], axis=1)


def sketch_kernel(steps, taps, block, prev, after, low, high, probes, sketch, band, edges):
    i = pl.program_id(0)

    @pl.when(i == 0)
    def _():
        band[...] = band_of(taps[...])
        sketch[...] = jnp.zeros_like(sketch)

    cleaned = clean(
        jnp.where(i == 0, low[...], prev[...]),
        block[...],
        jnp.where(i == steps - 1, high[...], after[...]),
        band[...],
    )
    sketch[...] += jnp.dot(cleaned, probes[...], preferred_element_type=F32)

    width = edges.shape[1] // 2

    @pl.when(i == 0)
    def _():
        edges[:, :width] = cleaned[:, :width]

    @pl.when(i == steps - 1)
    def _():
        edges[:, width:] = cleaned[:, -width:]


ANY = pl.BlockSpec(memory_space=pl.ANY)


def whole(shape):
    return pl.BlockSpec(shape, lambda i: (0, 0))


def block_specs(rows, size, first, last):
    per = size // TILE
    return [
        pl.BlockSpec((rows, size), lambda i: (0, first + i)),
        pl.BlockSpec((rows, TILE), lambda i: (0, jnp.maximum((first + i) * per - 1, 0))),
        pl.BlockSpec((rows, TILE), lambda i: (0, jnp.minimum((first + i + 1) * per, last))),
    ]


def sketch_of(taps, spectra, low, high, probes, edge):
    rows, bins = spectra.shape
    size = math.gcd(bins, 8192)
    steps = bins // size
    columns = probes.shape[1]
    return pl.pallas_call(
        functools.partial(sketch_kernel, steps),
        grid=(steps,),
        in_specs=[whole(taps.shape)]
        + block_specs(rows, size, 0, bins // TILE - 1)
        + [whole(low.shape), whole(high.shape)]
        + [pl.BlockSpec((size, columns), lambda i: (i, 0))],
        out_specs=[
            whole((rows, columns)),
            whole((2 * WIDTH, WIDTH)),
            whole((rows, 2 * edge)),
        ],
        out_shape=[
            jax.ShapeDtypeStruct((rows, columns), F32),
            jax.ShapeDtypeStruct((2 * WIDTH, WIDTH), BF16),
            jax.ShapeDtypeStruct((rows, 2 * edge), BF16),
        ],
        cost_estimate=COST,
        compiler_params=params(48),
    )(taps, spectra, spectra, spectra, low, high, probes)


def total_kernel(*refs):
    refs[-1][...] = pairwise([part[...] for part in refs[:-1]])


def total_of(parts):
    return pl.pallas_call(
        total_kernel,
        in_specs=[VMEM] * len(parts),
        out_specs=VMEM,
        out_shape=jax.ShapeDtypeStruct(parts[0].shape, F32),
        cost_estimate=COST,
        compiler_params=params(32),
    )(*parts)


def inverse_factor(gram):
    size = gram.shape[0]
    groups = range(size // 8)
    rows = [gram[8 * g : 8 * g + 8] for g in groups]
    lane = lax.broadcasted_iota(jnp.int32, (8, size), 1)
    sub = lax.broadcasted_iota(jnp.int32, (8, size), 0)

    def row_of(x, k):
        return jnp.broadcast_to(x[k : k + 1], (8, size))

    result = []
    for g in groups:
        inside = (lane >= 8 * g) & (lane < 8 * g + 8)
        below = groups[g:]
        cols = {
            h: [
                jnp.broadcast_to(rows[h][:, 8 * g + k : 8 * g + k + 1], (8, size))
                for k in range(8)
            ]
            for h in below
        }
        for h in below:
            unit = jnp.where(lane - 8 * g == sub, 1.0, 0.0) if h == g else 0.0
            rows[h] = jnp.where(inside, unit, rows[h])
        pivots = jnp.ones((8, size), F32)
        for k in range(8):
            pivot = row_of(cols[g][k], k)
            scale = 1.0 / pivot
            pivots = jnp.where(sub == k, pivot, pivots)
            line = row_of(rows[g], k) * scale
            heads = {m: row_of(cols[g][m], k) * scale for m in range(k + 1, 8)}
            for h in below:
                c = cols[h][k]
                if h == g:
                    c = jnp.where(sub > k, c, 0.0)
                rows[h] = rows[h] - c * line
                for m in range(k + 1, 8):
                    cols[h][m] = cols[h][m] - c * heads[m]
        result.append(jnp.where(lane < 8 * g + 8, rows[g] * lax.rsqrt(pivots), 0.0))
    return jnp.concatenate(result, axis=0)


def basis_kernel(chips, factor, count, *refs):
    own, near, basis, turned = refs[count : count + 4]
    outs, held, sems = refs[count + 4 : -2], refs[-2], refs[-1]
    rows, edge = held.shape[0] // 2, held.shape[1]
    copies = [
        pltpu.make_async_copy(
            one, held.at[pl.ds(n * rows, rows), :], sems.at[n]
        )
        for n, one in enumerate((own, near))
    ]
    for copy in copies:
        copy.start()
    sketches = [ref[...] for ref in refs[:count]]
    size = sketches[0].shape[1]
    grams = [
        lax.dot_general(
            one, one, (((0,), (0,)), ((), ())), precision=HIGHEST, preferred_element_type=F32
        )
        for one in sketches
    ]
    inverse = inverse_factor(pairwise(grams) / float(rows * len(sketches)))
    both = jnp.concatenate(sketches[:2], axis=0)
    across = lax.dot_general(
        inverse, both, (((1,), (1,)), ((), ())), precision=HIGHEST, preferred_element_type=F32
    )
    basis[...] = across[:, :rows].T.astype(BF16)
    share = size // (2 * chips)
    me = lax.axis_index("pix")
    shape = (size // 2, size)
    to = lax.broadcasted_iota(jnp.int32, shape, 0)
    source = lax.broadcasted_iota(jnp.int32, shape, 1)
    chip = lax.rem(to // share + me // 2, chips)
    wanted = (2 * chip + lax.rem(me, 2)) * share + lax.rem(to, share)
    pick = jnp.where(wanted == source, 1.0, 0.0).astype(BF16)
    turned[...] = jnp.dot(pick, across.astype(BF16), preferred_element_type=F32).astype(BF16)
    for copy in copies:
        copy.wait()
    for n in range(2):
        side = slice(n * edge // 2, (n + 1) * edge // 2)
        put_parts(turned, held[:, side], factor, outs[n * chips : (n + 1) * chips])


def basis_of(sketches, own, near, factor, chips):
    rows, size = sketches[0].shape
    edge = own.shape[1]
    share = size // (2 * chips)
    return pl.pallas_call(
        functools.partial(basis_kernel, chips, factor, len(sketches)),
        in_specs=[VMEM] * len(sketches) + [ANY] * 2,
        out_specs=[VMEM] * (2 + 2 * chips),
        out_shape=[
            jax.ShapeDtypeStruct((rows, size), BF16),
            jax.ShapeDtypeStruct((size // 2, 2 * rows), BF16),
        ]
        + [jax.ShapeDtypeStruct((share, edge // 2), BF16)] * (2 * chips),
        scratch_shapes=[
            pltpu.VMEM((2 * rows, edge), BF16),
            pltpu.SemaphoreType.DMA((2,)),
        ],
        cost_estimate=COST,
        compiler_params=params(32),
    )(*sketches, own, near)


def put_parts(turned, cleaned, factor, outs):
    used = cleaned.shape[0]
    part = jnp.dot(turned[:, :used], cleaned, preferred_element_type=F32) * factor
    share = outs[0].shape[0]
    for k, out in enumerate(outs):
        out[...] = part[k * share : (k + 1) * share].astype(BF16)


def project_kernel(factor, chips, turned, band, *refs):
    blocks, outs, done = refs[:6], refs[-1 - 2 * chips : -1], refs[-1]
    done[...] = jnp.zeros_like(done)
    cleaned = clean_all(blocks, band[...])

    @pl.when(pl.program_id(0) == 0)
    def _():
        put_parts(turned, cleaned, factor, outs[:chips])

    @pl.when(pl.program_id(0) == 1)
    def _():
        put_parts(turned, cleaned, factor, outs[chips:])


def clean_all(blocks, band):
    return jnp.concatenate(
        [
            clean(blocks[n + 1][...], blocks[n][...], blocks[n + 2][...], band)
            for n in range(0, len(blocks), 3)
        ],
        axis=0,
    )


def project(turned, band, spectra, near, start, size, factor, chips, wait):
    rows, bins = spectra.shape
    share = turned.shape[0] // chips
    return pl.pallas_call(
        functools.partial(project_kernel, factor, chips),
        grid=(2,),
        in_specs=[whole(turned.shape), whole(band.shape)]
        + block_specs(rows, size, start // size, bins // TILE - 1) * 2
        + [ANY] * len(wait),
        out_specs=[whole((share, size))] * (2 * chips) + [whole((8, TILE))],
        out_shape=[jax.ShapeDtypeStruct((share, size), BF16)] * (2 * chips)
        + [jax.ShapeDtypeStruct((8, TILE), F32)],
        cost_estimate=COST,
        compiler_params=params(50),
    )(turned, band, spectra, spectra, spectra, near, near, near, *wait)


def finish_kernel(blocks, count, *refs):
    out, done = refs[-2], refs[-1]
    done[...] = jnp.zeros_like(done)
    for n in range(blocks):

        @pl.when(pl.program_id(0) == n)
        def _():
            parts = refs[n * count : (n + 1) * count]
            out[...] = pairwise([part[...].astype(F32) for part in parts]).astype(BF16)


def finish(out, blocks, starts, bins, wait):
    parts = [part for block in blocks for part in block]
    share, size = parts[0].shape
    extra = [] if out is None else [out]
    return pl.pallas_call(
        functools.partial(finish_kernel, len(blocks), len(blocks[0])),
        grid=(len(blocks),),
        in_specs=[whole((share, size))] * len(parts) + [ANY] * (len(extra) + len(wait)),
        out_specs=[
            pl.BlockSpec(
                (share, size), lambda i: (0, jnp.where(i == 0, *[at // size for at in starts]))
            ),
            whole((8, TILE)),
        ],
        out_shape=[
            jax.ShapeDtypeStruct((share, bins), BF16),
            jax.ShapeDtypeStruct((8, TILE), F32),
        ],
        input_output_aliases={len(parts): 0} if extra else {},
        cost_estimate=COST,
        compiler_params=params(32),
    )(*parts, *extra, *wait)


def per_device(spectra, kernel, probes):
    rows, bins = spectra.shape
    pix = lax.axis_size("pix")
    depth = lax.axis_size("mz")
    chips = pix // 2
    factor = 1.0 / math.sqrt(float(rows * pix))

    up = [(i, i + 1) for i in range(depth - 1)]
    down = [(i + 1, i) for i in range(depth - 1)]
    low = lax.ppermute(spectra[:, bins - TILE :], "mz", up)
    high = lax.ppermute(spectra[:, :TILE], "mz", down)
    taps = jnp.pad(kernel.astype(F32), (REACH, 2 * WIDTH - REACH - kernel.shape[0]))[None]

    near = partner(spectra, "pix", 1)
    edge = math.gcd(bins // 2, EDGE)
    partial_sketch, band, edges = sketch_of(taps, spectra, low, high, probes, edge)
    near_edges = partner(edges, "pix", 1)
    sketch = total_of(spread(partial_sketch, "mz"))
    basis, turned, *mine = basis_of(
        gather(sketch, "pix"), edges, near_edges, factor, chips
    )

    routes = [
        [
            (2 * chip + core, 2 * ((chip + k) % chips) + core)
            for chip in range(chips)
            for core in range(2)
        ]
        for k in range(chips)
    ]

    def across(mine):
        return [mine[0]] + [lax.ppermute(mine[m], "pix", routes[m]) for m in range(1, chips)]

    def across(mine):
        return [mine[0]] + [lax.ppermute(mine[m], "pix", routes[m]) for m in range(1, chips)]

    out, recent = None, []
    before = ([across(mine[:chips]), across(mine[chips:])], (0, bins - edge))
    for start in range(edge, bins - edge, 2 * edge):
        *mine, done = project(turned, band, spectra, near, start, edge, factor, chips, recent)
        blocks = [across(mine[:chips]), across(mine[chips:])]
        out, done = finish(out, *before, bins, [done])
        recent = [done]
        before = (blocks, (start, start + edge))
    out, done = finish(out, *before, bins, recent)
    return (basis, out)


def solution(mesh):
    in_specs = (P(("groups", "pix"), "mz"), P(), P("mz", None))
    out_specs = (P(("groups", "pix"), None), P(("groups", "pix"), "mz"))
    return jax.shard_map(
        per_device, mesh=mesh, in_specs=in_specs, out_specs=out_specs, check_vma=False
    )
```

```python
import functools
import math

import jax
import jax.numpy as jnp
from jax import lax
from jax.experimental import pallas as pl
from jax.experimental.pallas import tpu as pltpu
from jax.sharding import PartitionSpec as P

F32 = jnp.float32
BF16 = jnp.bfloat16
HIGHEST = lax.Precision.HIGHEST
TILE = 128
WIDTH = 256
REACH = 64
EDGE = 4096
VMEM = pl.BlockSpec(memory_space=pltpu.VMEM)


COST = pl.CostEstimate(flops=1, bytes_accessed=1, transcendentals=0)


def params(limit=56):
    return pltpu.CompilerParams(vmem_limit_bytes=limit * 2**20)


def partner(x, axis, shift):
    count = lax.axis_size(axis)
    return lax.ppermute(x, axis, [(i, i ^ shift) for i in range(count)])


def gather(x, axis):
    count = lax.axis_size(axis)
    if count & (count - 1):
        every = lax.all_gather(x, axis)
        return [every[k] for k in range(count)]
    return [x] + [partner(x, axis, shift) for shift in range(1, count)]


def spread(x, axis):
    count = lax.axis_size(axis)
    if count & (count - 1):
        return [lax.psum(x, axis)]
    shift = count // 2
    while shift >= 4:
        x = x + partner(x, axis, shift)
        shift //= 2
    if count >= 4:
        x = total_of([x, partner(x, axis, 1)], [])
    return [x, partner(x, axis, 2)]


def pairwise(parts):
    while len(parts) > 1:
        odd = [parts[-1]] if len(parts) % 2 else []
        parts = [a + b for a, b in zip(parts[::2], parts[1::2])] + odd
    return parts[0]


def band_of(taps):
    wide = jnp.broadcast_to(taps, (WIDTH, 2 * WIDTH))
    return pltpu.roll(wide, 0, 1, stride=1, stride_axis=0).T.astype(BF16)


def clean(before, block, after, band):
    ext = jnp.concatenate([before, block, after], axis=1)
    rows, bins = block.shape
    starts = range(0, bins, WIDTH)
    lhs = jnp.concatenate([ext[:, a : a + 2 * WIDTH] for a in starts], axis=0)
    base = jnp.dot(lhs, band, preferred_element_type=F32)
    mid = jnp.concatenate([block[:, a : a + WIDTH] for a in starts], axis=0)
    out = (mid.astype(F32) - base).astype(BF16)
    return jnp.concatenate([out[i * rows : (i + 1) * rows] for i in range(bins // WIDTH)], axis=1)


def sketch_kernel(steps, taps, block, prev, after, low, high, probes, sketch, band, first, final):
    i = pl.program_id(0)

    @pl.when(i == 0)
    def _():
        band[...] = band_of(taps[...])
        sketch[...] = jnp.zeros_like(sketch)

    cleaned = clean(
        jnp.where(i == 0, low[...], prev[...]),
        block[...],
        jnp.where(i == steps - 1, high[...], after[...]),
        band[...],
    )
    sketch[...] += jnp.dot(cleaned, probes[...], preferred_element_type=F32)

    width = first.shape[1]

    @pl.when(i == 0)
    def _():
        first[...] = cleaned[:, :width]

    @pl.when(i == steps - 1)
    def _():
        final[...] = cleaned[:, -width:]


ANY = pl.BlockSpec(memory_space=pl.ANY)


def whole(shape):
    return pl.BlockSpec(shape, lambda i: (0, 0))


def block_specs(rows, size, first, last):
    per = size // TILE
    return [
        pl.BlockSpec((rows, size), lambda i: (0, first + i)),
        pl.BlockSpec((rows, TILE), lambda i: (0, jnp.maximum((first + i) * per - 1, 0))),
        pl.BlockSpec((rows, TILE), lambda i: (0, jnp.minimum((first + i + 1) * per, last))),
    ]


def sketch_of(taps, spectra, low, high, probes, edge):
    rows, bins = spectra.shape
    size = math.gcd(bins, 8192)
    steps = bins // size
    columns = probes.shape[1]
    return pl.pallas_call(
        functools.partial(sketch_kernel, steps),
        grid=(steps,),
        in_specs=[whole(taps.shape)]
        + block_specs(rows, size, 0, bins // TILE - 1)
        + [whole(low.shape), whole(high.shape)]
        + [pl.BlockSpec((size, columns), lambda i: (i, 0))],
        out_specs=[
            whole((rows, columns)),
            whole((2 * WIDTH, WIDTH)),
            whole((rows, edge)),
            whole((rows, edge)),
        ],
        out_shape=[
            jax.ShapeDtypeStruct((rows, columns), F32),
            jax.ShapeDtypeStruct((2 * WIDTH, WIDTH), BF16),
            jax.ShapeDtypeStruct((rows, edge), BF16),
            jax.ShapeDtypeStruct((rows, edge), BF16),
        ],
        cost_estimate=COST,
        compiler_params=params(48),
    )(taps, spectra, spectra, spectra, low, high, probes)


def total_kernel(count, *refs):
    refs[-1][...] = pairwise([part[...] for part in refs[:count]])


def total_of(parts, wait):
    return pl.pallas_call(
        functools.partial(total_kernel, len(parts)),
        in_specs=[VMEM] * len(parts) + [ANY] * len(wait),
        out_specs=VMEM,
        out_shape=jax.ShapeDtypeStruct(parts[0].shape, F32),
        cost_estimate=COST,
        compiler_params=params(32),
    )(*parts, *wait)


def inverse_factor(gram):
    size = gram.shape[0]
    groups = range(size // 8)
    rows = [gram[8 * g : 8 * g + 8] for g in groups]
    lane = lax.broadcasted_iota(jnp.int32, (8, size), 1)
    sub = lax.broadcasted_iota(jnp.int32, (8, size), 0)

    def row_of(x, k):
        return jnp.broadcast_to(x[k : k + 1], (8, size))

    result = []
    for g in groups:
        inside = (lane >= 8 * g) & (lane < 8 * g + 8)
        below = groups[g:]
        cols = {
            h: [
                jnp.broadcast_to(rows[h][:, 8 * g + k : 8 * g + k + 1], (8, size))
                for k in range(8)
            ]
            for h in below
        }
        for h in below:
            unit = jnp.where(lane - 8 * g == sub, 1.0, 0.0) if h == g else 0.0
            rows[h] = jnp.where(inside, unit, rows[h])
        pivots = jnp.ones((8, size), F32)
        for k in range(8):
            pivot = row_of(cols[g][k], k)
            scale = 1.0 / pivot
            pivots = jnp.where(sub == k, pivot, pivots)
            line = row_of(rows[g], k) * scale
            heads = {m: row_of(cols[g][m], k) * scale for m in range(k + 1, 8)}
            for h in below:
                c = cols[h][k]
                if h == g:
                    c = jnp.where(sub > k, c, 0.0)
                rows[h] = rows[h] - c * line
                for m in range(k + 1, 8):
                    cols[h][m] = cols[h][m] - c * heads[m]
        result.append(jnp.where(lane < 8 * g + 8, rows[g] * lax.rsqrt(pivots), 0.0))
    return jnp.concatenate(result, axis=0)


def basis_kernel(chips, factor, count, *refs):
    ends, (basis, turned) = refs[count : count + 4], refs[count + 4 : count + 6]
    outs, held, sems = refs[count + 6 : -2], refs[-2], refs[-1]
    rows = held.shape[1] // 2
    copies = [
        pltpu.make_async_copy(
            one, held.at[n // 2, pl.ds(n % 2 * rows, rows), :], sems.at[n]
        )
        for n, one in enumerate(ends)
    ]
    for copy in copies:
        copy.start()
    sketches = [ref[...] for ref in refs[:count]]
    size = sketches[0].shape[1]
    grams = [
        lax.dot_general(
            one, one, (((0,), (0,)), ((), ())), precision=HIGHEST, preferred_element_type=F32
        )
        for one in sketches
    ]
    inverse = inverse_factor(pairwise(grams) / float(rows * len(sketches)))
    both = jnp.concatenate(sketches[: turned.shape[1] // rows], axis=0)
    across = lax.dot_general(
        inverse, both, (((1,), (1,)), ((), ())), precision=HIGHEST, preferred_element_type=F32
    )
    basis[...] = across[:, :rows].T.astype(BF16)
    share = size // (2 * chips)
    me = lax.axis_index("pix")
    shape = (size // 2, size)
    to = lax.broadcasted_iota(jnp.int32, shape, 0)
    source = lax.broadcasted_iota(jnp.int32, shape, 1)
    chip = lax.rem(to // share + me // 2, chips)
    wanted = (2 * chip + lax.rem(me, 2)) * share + lax.rem(to, share)
    pick = jnp.where(wanted == source, 1.0, 0.0).astype(BF16)
    turned[...] = jnp.dot(pick, across.astype(BF16), preferred_element_type=F32).astype(BF16)
    for copy in copies:
        copy.wait()
    for n in range(2):
        put_parts(turned, held[n], factor, outs[n * chips : (n + 1) * chips])


def basis_of(sketches, ends, factor, chips, used):
    rows, size = sketches[0].shape
    edge = ends[0].shape[1]
    share = size // (2 * chips)
    return pl.pallas_call(
        functools.partial(basis_kernel, chips, factor, len(sketches)),
        in_specs=[VMEM] * len(sketches) + [ANY] * 4,
        out_specs=[VMEM] * (2 + 2 * chips),
        out_shape=[
            jax.ShapeDtypeStruct((rows, size), BF16),
            jax.ShapeDtypeStruct((size // 2, used * rows), BF16),
        ]
        + [jax.ShapeDtypeStruct((share, edge), BF16)] * (2 * chips),
        scratch_shapes=[
            pltpu.VMEM((2, 2 * rows, edge), BF16),
            pltpu.SemaphoreType.DMA((4,)),
        ],
        cost_estimate=COST,
        compiler_params=params(32),
    )(*sketches, *ends)


def put_parts(turned, cleaned, factor, outs):
    part = jnp.dot(turned[:, : cleaned.shape[0]], cleaned, preferred_element_type=F32) * factor
    share = outs[0].shape[0]
    for k, out in enumerate(outs):
        out[...] = part[k * share : (k + 1) * share].astype(BF16)


def project_kernel(count, factor, chips, turned, band, *refs):
    blocks, outs, done = refs[:6], refs[-1 - count * chips : -1], refs[-1]
    done[...] = jnp.zeros_like(done)
    cleaned = clean_all(blocks, band[...])
    for n in range(count):

        @pl.when(pl.program_id(0) == n)
        def _():
            put_parts(turned, cleaned, factor, outs[n * chips : (n + 1) * chips])


def clean_all(blocks, band):
    return jnp.concatenate(
        [
            clean(blocks[n + 1][...], blocks[n][...], blocks[n + 2][...], band)
            for n in range(0, len(blocks), 3)
        ],
        axis=0,
    )


def project(turned, band, spectra, near, start, size, count, factor, chips, wait):
    rows, bins = spectra.shape
    share = turned.shape[0] // chips
    return pl.pallas_call(
        functools.partial(project_kernel, count, factor, chips),
        grid=(count,),
        in_specs=[whole(turned.shape), whole(band.shape)]
        + block_specs(rows, size, start // size, bins // TILE - 1) * 2
        + [ANY] * len(wait),
        out_specs=[whole((share, size))] * (count * chips) + [whole((8, TILE))],
        out_shape=[jax.ShapeDtypeStruct((share, size), BF16)] * (count * chips)
        + [jax.ShapeDtypeStruct((8, TILE), F32)],
        cost_estimate=COST,
        compiler_params=params(50),
    )(turned, band, spectra, spectra, spectra, near, near, near, *wait)


def project_whole_kernel(factor, turned, band, own, own_low, own_high, near, *refs):
    near_low, near_high, far, other = refs[:4]
    out, done = refs[-2], refs[-1]
    done[...] = jnp.zeros_like(done)
    taps = band[...]
    cleaned = [
        clean(own_low[...], own[...], own_high[...], taps),
        clean(near_low[...], near[...], near_high[...], taps),
    ]
    for one in (far, other):
        last = one.shape[1] - TILE
        cleaned.append(clean(one[:, :TILE], one[:, TILE:last], one[:, last:], taps))
    put_parts(turned.at[: out.shape[0]], jnp.concatenate(cleaned, axis=0), factor, [out])


def project_whole(out, turned, band, spectra, near, far, start, factor, wait):
    rows, bins = spectra.shape
    size = far[0].shape[1] - 2 * TILE
    first = start // size
    return pl.pallas_call(
        functools.partial(project_whole_kernel, factor),
        grid=(1,),
        in_specs=[whole(turned.shape), whole(band.shape)]
        + block_specs(rows, size, first, bins // TILE - 1) * 2
        + [whole(one.shape) for one in far]
        + [ANY] * (1 + len(wait)),
        out_specs=[pl.BlockSpec((out.shape[0], size), lambda i: (0, first)), whole((8, TILE))],
        out_shape=[
            jax.ShapeDtypeStruct(out.shape, BF16),
            jax.ShapeDtypeStruct((8, TILE), F32),
        ],
        input_output_aliases={10: 0},
        cost_estimate=COST,
        compiler_params=params(50),
    )(turned, band, *[spectra] * 3, *[near] * 3, *far, out, *wait)


def finish_kernel(blocks, count, *refs):
    out, done = refs[-2], refs[-1]
    done[...] = jnp.zeros_like(done)
    for n in range(blocks):

        @pl.when(pl.program_id(0) == n)
        def _():
            parts = refs[n * count : (n + 1) * count]
            out[...] = pairwise([part[...].astype(F32) for part in parts]).astype(BF16)


def finish(out, blocks, starts, bins, wait):
    parts = [part for block in blocks for part in block]
    share, size = parts[0].shape
    extra = [] if out is None else [out]
    return pl.pallas_call(
        functools.partial(finish_kernel, len(blocks), len(blocks[0])),
        grid=(len(blocks),),
        in_specs=[whole((share, size))] * len(parts) + [ANY] * (len(extra) + len(wait)),
        out_specs=[
            pl.BlockSpec(
                (share, size),
                lambda i: (0, jnp.where(i == 0, starts[0] // size, starts[-1] // size)),
            ),
            whole((8, TILE)),
        ],
        out_shape=[
            jax.ShapeDtypeStruct((share, bins), BF16),
            jax.ShapeDtypeStruct((8, TILE), F32),
        ],
        input_output_aliases={len(parts): 0} if extra else {},
        cost_estimate=COST,
        compiler_params=params(32),
    )(*parts, *extra, *wait)


def per_device(spectra, kernel, probes):
    rows, bins = spectra.shape
    pix = lax.axis_size("pix")
    depth = lax.axis_size("mz")
    chips = pix // 2
    factor = 1.0 / math.sqrt(float(rows * pix))

    up = [(i, i + 1) for i in range(depth - 1)]
    down = [(i + 1, i) for i in range(depth - 1)]
    low = lax.ppermute(spectra[:, bins - TILE :], "mz", up)
    high = lax.ppermute(spectra[:, :TILE], "mz", down)
    taps = jnp.pad(kernel.astype(F32), (REACH, 2 * WIDTH - REACH - kernel.shape[0]))[None]

    near = partner(spectra, "pix", 1)
    edge = math.gcd(bins // 2, EDGE)
    far = []
    inner = edge
    if chips == 2 and bins >= 6 * edge:
        far = [partner(spectra[:, edge - TILE : 2 * edge + TILE], "pix", 2)]
        inner = 2 * edge
    partial_sketch, band, first, final = sketch_of(taps, spectra, low, high, probes, edge)
    ends = [first, partner(first, "pix", 1), final, partner(final, "pix", 1)]
    sketch = total_of(spread(partial_sketch, "mz"), far)
    basis, turned, *mine = basis_of(
        gather(sketch, "pix"), ends, factor, chips, 2 + 2 * len(far)
    )

    routes = [
        [
            (2 * chip + core, 2 * ((chip + k) % chips) + core)
            for chip in range(chips)
            for core in range(2)
        ]
        for k in range(chips)
    ]

    def across(mine):
        return [mine[0]] + [lax.ppermute(mine[m], "pix", routes[m]) for m in range(1, chips)]

    def across(mine):
        return [mine[0]] + [lax.ppermute(mine[m], "pix", routes[m]) for m in range(1, chips)]

    out, recent = None, []
    before = ([across(mine[:chips]), across(mine[chips:])], (0, bins - edge))
    for start in range(inner, bins - edge, 2 * edge):
        count = min(2, (bins - edge - start) // edge)
        *mine, done = project(
            turned, band, spectra, near, start, edge, count, factor, chips, recent
        )
        blocks = [across(mine[n * chips : (n + 1) * chips]) for n in range(count)]
        recent = [done]
        if far and start + count * edge == bins - edge:
            pair = [far[0], partner(far[0], "pix", 1)]
            out, done = project_whole(
                out, turned, band, spectra, near, pair, edge, factor, recent
            )
            recent = [done]
        out, done = finish(out, *before, bins, recent)
        recent = [done]
        before = (blocks, tuple(start + n * edge for n in range(count)))
    out, done = finish(out, *before, bins, recent)
    return (basis, out)


def solution(mesh):
    in_specs = (P(("groups", "pix"), "mz"), P(), P("mz", None))
    out_specs = (P(("groups", "pix"), None), P(("groups", "pix"), "mz"))
    return jax.shard_map(
        per_device, mesh=mesh, in_specs=in_specs, out_specs=out_specs, check_vma=False
    )
```

```python
import functools
import math

import jax
import jax.numpy as jnp
from jax import lax
from jax.experimental import pallas as pl
from jax.experimental.pallas import tpu as pltpu
from jax.sharding import PartitionSpec as P

F32 = jnp.float32
BF16 = jnp.bfloat16
HIGHEST = lax.Precision.HIGHEST
TILE = 128
WIDTH = 256
REACH = 64
EDGE = 4096
EARLY = 4096
VMEM = pl.BlockSpec(memory_space=pltpu.VMEM)


COST = pl.CostEstimate(flops=1, bytes_accessed=1, transcendentals=0)


def params(limit=56):
    return pltpu.CompilerParams(vmem_limit_bytes=limit * 2**20)


def partner(x, axis, shift):
    count = lax.axis_size(axis)
    return lax.ppermute(x, axis, [(i, i ^ shift) for i in range(count)])


def gather(x, axis):
    count = lax.axis_size(axis)
    if count & (count - 1):
        every = lax.all_gather(x, axis)
        return [every[k] for k in range(count)]
    return [x] + [partner(x, axis, shift) for shift in range(1, count)]


def spread(x, axis):
    count = lax.axis_size(axis)
    if count & (count - 1):
        return [lax.psum(x, axis)]
    shift = count // 2
    while shift >= 4:
        x = x + partner(x, axis, shift)
        shift //= 2
    if count >= 4:
        x = total_of([x, partner(x, axis, 1)], [])
    return [x, partner(x, axis, 2)]


def pairwise(parts):
    while len(parts) > 1:
        odd = [parts[-1]] if len(parts) % 2 else []
        parts = [a + b for a, b in zip(parts[::2], parts[1::2])] + odd
    return parts[0]


def band_of(taps):
    wide = jnp.broadcast_to(taps, (WIDTH, 2 * WIDTH))
    return pltpu.roll(wide, 0, 1, stride=1, stride_axis=0).T.astype(BF16)


def clean(before, block, after, band):
    ext = jnp.concatenate([before, block, after], axis=1)
    rows, bins = block.shape
    starts = range(0, bins, WIDTH)
    lhs = jnp.concatenate([ext[:, a : a + 2 * WIDTH] for a in starts], axis=0)
    base = jnp.dot(lhs, band, preferred_element_type=F32)
    mid = jnp.concatenate([block[:, a : a + WIDTH] for a in starts], axis=0)
    out = (mid.astype(F32) - base).astype(BF16)
    return jnp.concatenate([out[i * rows : (i + 1) * rows] for i in range(bins // WIDTH)], axis=1)


def sketch_kernel(steps, taps, block, prev, after, even, odd, probes, sketch, band, first, final):
    i = pl.program_id(0)
    lower = lax.rem(lax.axis_index("mz"), 2) == 0
    low = jnp.where(lower, odd[...], even[...])
    high = jnp.where(lower, even[...], odd[...])

    @pl.when(i == 0)
    def _():
        band[...] = band_of(taps[...])
        sketch[...] = jnp.zeros_like(sketch)

    cleaned = clean(
        jnp.where(i == 0, low, prev[...]),
        block[...],
        jnp.where(i == steps - 1, high, after[...]),
        band[...],
    )
    sketch[...] += jnp.dot(cleaned, probes[...], preferred_element_type=F32)

    width = first.shape[1]

    @pl.when(i == 0)
    def _():
        first[...] = cleaned[:, :width]

    @pl.when(i == steps - 1)
    def _():
        final[...] = cleaned[:, -width:]


ANY = pl.BlockSpec(memory_space=pl.ANY)


def whole(shape):
    return pl.BlockSpec(shape, lambda i: (0, 0))


def at(shape, place):
    return pl.BlockSpec(
        tuple(pl.Element(n) for n in shape), lambda i: (0, place(i) * TILE)
    )


def inner_specs(rows, size, start):
    first, per = start // TILE, size // TILE
    return [
        at((rows, size), lambda i: first + i * per),
        at((rows, TILE), lambda i: first + i * per - 1),
        at((rows, TILE), lambda i: first + i * per + per),
    ]


def block_specs(rows, size, first, last):
    per = size // TILE
    return [
        pl.BlockSpec((rows, size), lambda i: (0, first + i)),
        pl.BlockSpec((rows, TILE), lambda i: (0, jnp.maximum((first + i) * per - 1, 0))),
        pl.BlockSpec((rows, TILE), lambda i: (0, jnp.minimum((first + i + 1) * per, last))),
    ]


def sketch_of(taps, spectra, even, odd, probes, edge):
    rows, bins = spectra.shape
    size = math.gcd(bins, 8192)
    steps = bins // size
    columns = probes.shape[1]
    return pl.pallas_call(
        functools.partial(sketch_kernel, steps),
        grid=(steps,),
        in_specs=[whole(taps.shape)]
        + block_specs(rows, size, 0, bins // TILE - 1)
        + [whole(even.shape), whole(odd.shape)]
        + [pl.BlockSpec((size, columns), lambda i: (i, 0))],
        out_specs=[
            whole((rows, columns)),
            whole((2 * WIDTH, WIDTH)),
            whole((rows, edge)),
            whole((rows, edge)),
        ],
        out_shape=[
            jax.ShapeDtypeStruct((rows, columns), F32),
            jax.ShapeDtypeStruct((2 * WIDTH, WIDTH), BF16),
            jax.ShapeDtypeStruct((rows, edge), BF16),
            jax.ShapeDtypeStruct((rows, edge), BF16),
        ],
        cost_estimate=COST,
        compiler_params=params(48),
    )(taps, spectra, spectra, spectra, even, odd, probes)


def total_kernel(count, *refs):
    refs[-1][...] = pairwise([part[...] for part in refs[:count]])


def total_of(parts, wait):
    return pl.pallas_call(
        functools.partial(total_kernel, len(parts)),
        in_specs=[VMEM] * len(parts) + [ANY] * len(wait),
        out_specs=VMEM,
        out_shape=jax.ShapeDtypeStruct(parts[0].shape, F32),
        cost_estimate=COST,
        compiler_params=params(32),
    )(*parts, *wait)


def inverse_factor(gram):
    size = gram.shape[0]
    groups = range(size // 8)
    rows = [gram[8 * g : 8 * g + 8] for g in groups]
    lane = lax.broadcasted_iota(jnp.int32, (8, size), 1)
    sub = lax.broadcasted_iota(jnp.int32, (8, size), 0)

    def row_of(x, k):
        return jnp.broadcast_to(x[k : k + 1], (8, size))

    result = []
    for g in groups:
        inside = (lane >= 8 * g) & (lane < 8 * g + 8)
        below = groups[g:]
        cols = {
            h: [
                jnp.broadcast_to(rows[h][:, 8 * g + k : 8 * g + k + 1], (8, size))
                for k in range(8)
            ]
            for h in below
        }
        for h in below:
            unit = jnp.where(lane - 8 * g == sub, 1.0, 0.0) if h == g else 0.0
            rows[h] = jnp.where(inside, unit, rows[h])
        pivots = jnp.ones((8, size), F32)
        for k in range(8):
            pivot = row_of(cols[g][k], k)
            scale = 1.0 / pivot
            pivots = jnp.where(sub == k, pivot, pivots)
            line = row_of(rows[g], k) * scale
            heads = {m: row_of(cols[g][m], k) * scale for m in range(k + 1, 8)}
            for h in below:
                c = cols[h][k]
                if h == g:
                    c = jnp.where(sub > k, c, 0.0)
                rows[h] = rows[h] - c * line
                for m in range(k + 1, 8):
                    cols[h][m] = cols[h][m] - c * heads[m]
        result.append(jnp.where(lane < 8 * g + 8, rows[g] * lax.rsqrt(pivots), 0.0))
    return jnp.concatenate(result, axis=0)


def basis_kernel(chips, factor, count, *refs):
    ends, (basis, turned) = refs[count : count + 4], refs[count + 4 : count + 6]
    outs, held, sems = refs[count + 6 : -2], refs[-2], refs[-1]
    rows = held.shape[1] // 2
    copies = [
        pltpu.make_async_copy(
            one, held.at[n // 2, pl.ds(n % 2 * rows, rows), :], sems.at[n]
        )
        for n, one in enumerate(ends)
    ]
    for copy in copies:
        copy.start()
    sketches = [ref[...] for ref in refs[:count]]
    size = sketches[0].shape[1]
    stacked = jnp.concatenate(sketches, axis=0)
    gram = lax.dot_general(
        stacked, stacked, (((0,), (0,)), ((), ())), precision=HIGHEST, preferred_element_type=F32
    )
    inverse = inverse_factor(gram / float(stacked.shape[0]))
    used = stacked[: turned.shape[1]]
    across = lax.dot_general(
        inverse, used, (((1,), (1,)), ((), ())), precision=HIGHEST, preferred_element_type=F32
    )
    basis[...] = across[:, :rows].T.astype(BF16)
    share = size // (2 * chips)
    me = lax.axis_index("pix")
    shape = (size // 2, size)
    to = lax.broadcasted_iota(jnp.int32, shape, 0)
    source = lax.broadcasted_iota(jnp.int32, shape, 1)
    chip = lax.rem(to // share + me // 2, chips)
    wanted = (2 * chip + lax.rem(me, 2)) * share + lax.rem(to, share)
    pick = jnp.where(wanted == source, 1.0, 0.0).astype(BF16)
    turned[...] = jnp.dot(pick, across.astype(BF16), preferred_element_type=F32).astype(BF16)
    for copy in copies:
        copy.wait()
    for n in range(2):
        put_parts(turned, held[n], factor, outs[n * chips : (n + 1) * chips])


def basis_of(sketches, ends, factor, chips, used):
    rows, size = sketches[0].shape
    edge = ends[0].shape[1]
    share = size // (2 * chips)
    return pl.pallas_call(
        functools.partial(basis_kernel, chips, factor, len(sketches)),
        in_specs=[VMEM] * len(sketches) + [ANY] * 4,
        out_specs=[VMEM] * (2 + 2 * chips),
        out_shape=[
            jax.ShapeDtypeStruct((rows, size), BF16),
            jax.ShapeDtypeStruct((size // 2, used * rows), BF16),
        ]
        + [jax.ShapeDtypeStruct((share, edge), BF16)] * (2 * chips),
        scratch_shapes=[
            pltpu.VMEM((2, 2 * rows, edge), BF16),
            pltpu.SemaphoreType.DMA((4,)),
        ],
        cost_estimate=COST,
        compiler_params=params(32),
    )(*sketches, *ends)


def put_parts(turned, cleaned, factor, outs):
    part = jnp.dot(turned[:, : cleaned.shape[0]], cleaned, preferred_element_type=F32) * factor
    share = outs[0].shape[0]
    for k, out in enumerate(outs):
        out[...] = part[k * share : (k + 1) * share].astype(BF16)


def project_kernel(count, factor, chips, turned, band, *refs):
    blocks, outs, done = refs[:6], refs[-1 - count * chips : -1], refs[-1]
    done[...] = jnp.zeros_like(done)
    cleaned = clean_all(blocks, band[...])
    for n in range(count):

        @pl.when(pl.program_id(0) == n)
        def _():
            put_parts(turned, cleaned, factor, outs[n * chips : (n + 1) * chips])


def clean_all(blocks, band):
    return jnp.concatenate(
        [
            clean(blocks[n + 1][...], blocks[n][...], blocks[n + 2][...], band)
            for n in range(0, len(blocks), 3)
        ],
        axis=0,
    )


def project(turned, band, spectra, near, start, size, count, factor, chips, wait):
    rows = spectra.shape[0]
    share = turned.shape[0] // chips
    return pl.pallas_call(
        functools.partial(project_kernel, count, factor, chips),
        grid=(count,),
        in_specs=[whole(turned.shape), whole(band.shape)]
        + inner_specs(rows, size, start) * 2
        + [ANY] * len(wait),
        out_specs=[whole((share, size))] * (count * chips) + [whole((8, TILE))],
        out_shape=[jax.ShapeDtypeStruct((share, size), BF16)] * (count * chips)
        + [jax.ShapeDtypeStruct((8, TILE), F32)],
        cost_estimate=COST,
        compiler_params=params(50),
    )(turned, band, spectra, spectra, spectra, near, near, near, *wait)


def project_whole_kernel(factor, turned, band, own, own_low, own_high, near, *refs):
    near_low, near_high, far, other = refs[:4]
    out, done = refs[-2], refs[-1]
    done[...] = jnp.zeros_like(done)
    taps = band[...]
    cleaned = [
        clean(own_low[...], own[...], own_high[...], taps),
        clean(near_low[...], near[...], near_high[...], taps),
    ]
    for one in (far, other):
        last = one.shape[1] - TILE
        cleaned.append(clean(one[:, :TILE], one[:, TILE:last], one[:, last:], taps))
    put_parts(turned.at[: out.shape[0]], jnp.concatenate(cleaned, axis=0), factor, [out])


def project_whole(out, turned, band, spectra, near, far, start, factor, wait):
    rows = spectra.shape[0]
    size = far[0].shape[1] - 2 * TILE
    return pl.pallas_call(
        functools.partial(project_whole_kernel, factor),
        grid=(1,),
        in_specs=[whole(turned.shape), whole(band.shape)]
        + inner_specs(rows, size, start) * 2
        + [whole(one.shape) for one in far]
        + [ANY] * (1 + len(wait)),
        out_specs=[at((out.shape[0], size), lambda i: start // TILE), whole((8, TILE))],
        out_shape=[
            jax.ShapeDtypeStruct(out.shape, BF16),
            jax.ShapeDtypeStruct((8, TILE), F32),
        ],
        input_output_aliases={10: 0},
        cost_estimate=COST,
        compiler_params=params(50),
    )(turned, band, *[spectra] * 3, *[near] * 3, *far, out, *wait)


def finish_kernel(blocks, count, *refs):
    out, done = refs[-2], refs[-1]
    done[...] = jnp.zeros_like(done)
    for n in range(blocks):

        @pl.when(pl.program_id(0) == n)
        def _():
            parts = refs[n * count : (n + 1) * count]
            out[...] = pairwise([part[...].astype(F32) for part in parts]).astype(BF16)


def finish(out, blocks, starts, bins, wait):
    parts = [part for block in blocks for part in block]
    share, size = parts[0].shape
    extra = [] if out is None else [out]
    return pl.pallas_call(
        functools.partial(finish_kernel, len(blocks), len(blocks[0])),
        grid=(len(blocks),),
        in_specs=[whole((share, size))] * len(parts) + [ANY] * (len(extra) + len(wait)),
        out_specs=[
            at(
                (share, size),
                lambda i: jnp.where(i == 0, starts[0] // TILE, starts[-1] // TILE),
            ),
            whole((8, TILE)),
        ],
        out_shape=[
            jax.ShapeDtypeStruct((share, bins), BF16),
            jax.ShapeDtypeStruct((8, TILE), F32),
        ],
        input_output_aliases={len(parts): 0} if extra else {},
        cost_estimate=COST,
        compiler_params=params(32),
    )(*parts, *extra, *wait)


def per_device(spectra, kernel, probes):
    rows, bins = spectra.shape
    pix = lax.axis_size("pix")
    depth = lax.axis_size("mz")
    chips = pix // 2
    factor = 1.0 / math.sqrt(float(rows * pix))

    def swap(first, tile):
        pairs = [(i, i + 1) for i in range(first, depth - 1, 2)]
        return lax.ppermute(tile, "mz", pairs + [(b, a) for a, b in pairs])

    lower = lax.rem(lax.axis_index("mz"), 2) == 0
    head, tail = spectra[:, :TILE], spectra[:, bins - TILE :]
    even = swap(0, jnp.where(lower, tail, head))
    odd = swap(1, jnp.where(lower, head, tail))
    taps = jnp.pad(kernel.astype(F32), (REACH, 2 * WIDTH - REACH - kernel.shape[0]))[None]

    near = partner(spectra, "pix", 1)
    edge = math.gcd(bins // 2, EDGE)
    far = []
    inner = edge
    if chips == 2 and bins >= 8 * EARLY:
        inner = edge + EARLY
        far = [partner(spectra[:, edge - TILE : inner + TILE], "pix", 2)]
    partial_sketch, band, first, final = sketch_of(taps, spectra, even, odd, probes, edge)
    ends = [first, partner(first, "pix", 1), final, partner(final, "pix", 1)]
    sketch = total_of(spread(partial_sketch, "mz"), far)
    basis, turned, *mine = basis_of(
        gather(sketch, "pix"), ends, factor, chips, 2 + 2 * len(far)
    )

    routes = [
        [
            (2 * chip + core, 2 * ((chip + k) % chips) + core)
            for chip in range(chips)
            for core in range(2)
        ]
        for k in range(chips)
    ]

    def across(mine):
        return [mine[0]] + [lax.ppermute(mine[m], "pix", routes[m]) for m in range(1, chips)]

    def across(mine):
        return [mine[0]] + [lax.ppermute(mine[m], "pix", routes[m]) for m in range(1, chips)]

    out, recent = None, []
    before = ([across(mine[:chips]), across(mine[chips:])], (0, bins - edge))
    start, stop = inner, bins - edge
    while start < stop:
        size = min(edge, stop - start)
        count = min(2, (stop - start) // size)
        *mine, done = project(
            turned, band, spectra, near, start, size, count, factor, chips, recent
        )
        blocks = [across(mine[n * chips : (n + 1) * chips]) for n in range(count)]
        recent = [done]
        places = tuple(start + n * size for n in range(count))
        start += count * size
        if far and start == stop:
            pair = [far[0], partner(far[0], "pix", 1)]
            out, done = project_whole(
                out, turned, band, spectra, near, pair, edge, factor, recent
            )
            recent = [done]
        out, done = finish(out, *before, bins, recent)
        recent = [done]
        before = (blocks, places)
    out, done = finish(out, *before, bins, recent)
    return (basis, out)


def solution(mesh):
    in_specs = (P(("groups", "pix"), "mz"), P(), P("mz", None))
    out_specs = (P(("groups", "pix"), None), P(("groups", "pix"), "mz"))
    return jax.shard_map(
        per_device, mesh=mesh, in_specs=in_specs, out_specs=out_specs, check_vma=False
    )
```

```python
import functools
import math

import jax
import jax.numpy as jnp
from jax import lax
from jax.experimental import pallas as pl
from jax.experimental.pallas import tpu as pltpu
from jax.sharding import PartitionSpec as P

F32 = jnp.float32
BF16 = jnp.bfloat16
HIGHEST = lax.Precision.HIGHEST
TILE = 128
WIDTH = 256
REACH = 64
EDGE = 4096
EARLY = 4096
VMEM = pl.BlockSpec(memory_space=pltpu.VMEM)


COST = pl.CostEstimate(flops=1, bytes_accessed=1, transcendentals=0)


def params(limit=56):
    return pltpu.CompilerParams(vmem_limit_bytes=limit * 2**20)


def partner(x, axis, shift):
    count = lax.axis_size(axis)
    return lax.ppermute(x, axis, [(i, i ^ shift) for i in range(count)])


def gather(x, axis):
    count = lax.axis_size(axis)
    if count & (count - 1):
        every = lax.all_gather(x, axis)
        return [every[k] for k in range(count)]
    return [x] + [partner(x, axis, shift) for shift in range(1, count)]


def spread(x, axis):
    count = lax.axis_size(axis)
    if count & (count - 1):
        return [lax.psum(x, axis)]
    shift = count // 2
    while shift >= 4:
        x = x + partner(x, axis, shift)
        shift //= 2
    if count >= 4:
        x = total_of([x, partner(x, axis, 1)], [])
    return [x, partner(x, axis, 2)]


def pairwise(parts):
    while len(parts) > 1:
        odd = [parts[-1]] if len(parts) % 2 else []
        parts = [a + b for a, b in zip(parts[::2], parts[1::2])] + odd
    return parts[0]


def band_of(taps):
    wide = jnp.broadcast_to(taps, (WIDTH, 2 * WIDTH))
    return pltpu.roll(wide, 0, 1, stride=1, stride_axis=0).T.astype(BF16)


def clean(before, block, after, band):
    ext = jnp.concatenate([before, block, after], axis=1)
    rows, bins = block.shape
    starts = range(0, bins, WIDTH)
    lhs = jnp.concatenate([ext[:, a : a + 2 * WIDTH] for a in starts], axis=0)
    base = jnp.dot(lhs, band, preferred_element_type=F32)
    mid = jnp.concatenate([block[:, a : a + WIDTH] for a in starts], axis=0)
    out = (mid.astype(F32) - base).astype(BF16)
    return jnp.concatenate([out[i * rows : (i + 1) * rows] for i in range(bins // WIDTH)], axis=1)


def sketch_kernel(steps, taps, even, odd, spectra, probes, *refs):
    sketch, band, first, final, ext, held, one, two, came, there = refs
    size = one.shape[1]
    bins = steps * size

    def bins_copy(c):
        start = pl.multiple_of(c * size, size)
        return pltpu.make_async_copy(
            spectra.at[:, pl.ds(start, size)], ext.at[:, pl.ds(start + TILE, size)], came.at[c]
        )

    def probes_copy(c):
        start = pl.multiple_of(c * size, size)
        return pltpu.make_async_copy(
            probes.at[pl.ds(start, size), :], held.at[pl.ds(start, size), :], there.at[c]
        )

    for c in range(steps):
        bins_copy(c).start()
        if c > 0:
            probes_copy(c - 1).start()
    probes_copy(steps - 1).start()
    lower = lax.rem(lax.axis_index("mz"), 2) == 0
    ext[:, :TILE] = jnp.where(lower, odd[...], even[...])
    ext[:, bins + TILE :] = jnp.where(lower, even[...], odd[...])
    band[...] = band_of(taps[...])
    sketch[...] = jnp.zeros_like(sketch)

    def filter_to(out, c):
        start = pl.multiple_of(c * size, size)

        def part(a, b):
            return ext[:, pl.ds(pl.multiple_of(start + a, TILE), b - a)]

        for a in range(0, size, WIDTH):
            base = jnp.dot(part(a, a + 2 * WIDTH), band[...], preferred_element_type=F32)
            block = part(a + TILE, a + TILE + WIDTH).astype(F32)
            out[:, a : a + WIDTH] = (block - base).astype(BF16)

    def add(cleaned, c):
        rows = held[pl.ds(pl.multiple_of(c * size, size), size), :]
        sketch[...] += jnp.dot(cleaned[...], rows, preferred_element_type=F32)

    bins_copy(0).wait()
    bins_copy(1).wait()
    filter_to(one, 0)
    first[...] = one[:, : first.shape[1]]
    probes_copy(0).wait()

    def pair(k, carry):
        c = 2 * k + 1

        @pl.when(c + 1 < steps)
        def _():
            bins_copy(c + 1).wait()

        filter_to(two, c)
        add(one, c - 1)
        probes_copy(c).wait()

        @pl.when(c + 1 < steps)
        def _():
            bins_copy(c + 2).wait()
            filter_to(one, c + 1)
            add(two, c)
            probes_copy(c + 1).wait()

        return carry

    lax.fori_loop(0, steps // 2, pair, 0)
    add(two, steps - 1)
    final[...] = two[:, size - final.shape[1] :]


ANY = pl.BlockSpec(memory_space=pl.ANY)


def whole(shape):
    return pl.BlockSpec(shape, lambda i: (0, 0))


def at(shape, place):
    return pl.BlockSpec(
        tuple(pl.Element(n) for n in shape), lambda i: (0, place(i) * TILE)
    )


def inner_specs(rows, size, start):
    first, per = start // TILE, size // TILE
    return [
        at((rows, size), lambda i: first + i * per),
        at((rows, TILE), lambda i: first + i * per - 1),
        at((rows, TILE), lambda i: first + i * per + per),
    ]


def block_specs(rows, size, first, last):
    per = size // TILE
    return [
        pl.BlockSpec((rows, size), lambda i: (0, first + i)),
        pl.BlockSpec((rows, TILE), lambda i: (0, jnp.maximum((first + i) * per - 1, 0))),
        pl.BlockSpec((rows, TILE), lambda i: (0, jnp.minimum((first + i + 1) * per, last))),
    ]


def sketch_of(taps, spectra, even, odd, probes, edge):
    rows, bins = spectra.shape
    size = math.gcd(bins // 2, 8192)
    steps = bins // size
    columns = probes.shape[1]
    return pl.pallas_call(
        functools.partial(sketch_kernel, steps),
        in_specs=[VMEM] * 3 + [ANY] * 2,
        out_specs=[VMEM] * 4,
        out_shape=[
            jax.ShapeDtypeStruct((rows, columns), F32),
            jax.ShapeDtypeStruct((2 * WIDTH, WIDTH), BF16),
            jax.ShapeDtypeStruct((rows, edge), BF16),
            jax.ShapeDtypeStruct((rows, edge), BF16),
        ],
        scratch_shapes=[
            pltpu.VMEM((rows, bins + 2 * TILE), BF16),
            pltpu.VMEM((bins, columns), BF16),
            pltpu.VMEM((rows, size), BF16),
            pltpu.VMEM((rows, size), BF16),
            pltpu.SemaphoreType.DMA((steps,)),
            pltpu.SemaphoreType.DMA((steps,)),
        ],
        cost_estimate=COST,
        compiler_params=params(50),
    )(taps, even, odd, spectra, probes)


def total_kernel(count, *refs):
    refs[-1][...] = pairwise([part[...] for part in refs[:count]])


def total_of(parts, wait):
    return pl.pallas_call(
        functools.partial(total_kernel, len(parts)),
        in_specs=[VMEM] * len(parts) + [ANY] * len(wait),
        out_specs=VMEM,
        out_shape=jax.ShapeDtypeStruct(parts[0].shape, F32),
        cost_estimate=COST,
        compiler_params=params(32),
    )(*parts, *wait)


def inverse_factor(gram):
    size = gram.shape[0]
    groups = range(size // 8)
    rows = [gram[8 * g : 8 * g + 8] for g in groups]
    lane = lax.broadcasted_iota(jnp.int32, (8, size), 1)
    sub = lax.broadcasted_iota(jnp.int32, (8, size), 0)

    def row_of(x, k):
        return jnp.broadcast_to(x[k : k + 1], (8, size))

    result = []
    for g in groups:
        inside = (lane >= 8 * g) & (lane < 8 * g + 8)
        below = groups[g:]
        cols = {
            h: [
                jnp.broadcast_to(rows[h][:, 8 * g + k : 8 * g + k + 1], (8, size))
                for k in range(8)
            ]
            for h in below
        }
        for h in below:
            unit = jnp.where(lane - 8 * g == sub, 1.0, 0.0) if h == g else 0.0
            rows[h] = jnp.where(inside, unit, rows[h])
        pivots = jnp.ones((8, size), F32)
        for k in range(8):
            pivot = row_of(cols[g][k], k)
            scale = 1.0 / pivot
            pivots = jnp.where(sub == k, pivot, pivots)
            line = row_of(rows[g], k) * scale
            heads = {m: row_of(cols[g][m], k) * scale for m in range(k + 1, 8)}
            for h in below:
                c = cols[h][k]
                if h == g:
                    c = jnp.where(sub > k, c, 0.0)
                rows[h] = rows[h] - c * line
                for m in range(k + 1, 8):
                    cols[h][m] = cols[h][m] - c * heads[m]
        result.append(jnp.where(lane < 8 * g + 8, rows[g] * lax.rsqrt(pivots), 0.0))
    return jnp.concatenate(result, axis=0)


def basis_kernel(chips, factor, count, *refs):
    ends, (basis, turned) = refs[count : count + 4], refs[count + 4 : count + 6]
    outs, held, sems = refs[count + 6 : -2], refs[-2], refs[-1]
    rows = held.shape[1] // 2
    copies = [
        pltpu.make_async_copy(
            one, held.at[n // 2, pl.ds(n % 2 * rows, rows), :], sems.at[n]
        )
        for n, one in enumerate(ends)
    ]
    for copy in copies:
        copy.start()
    sketches = [ref[...] for ref in refs[:count]]
    size = sketches[0].shape[1]
    stacked = jnp.concatenate(sketches, axis=0)
    gram = lax.dot_general(
        stacked, stacked, (((0,), (0,)), ((), ())), precision=HIGHEST, preferred_element_type=F32
    )
    inverse = inverse_factor(gram / float(stacked.shape[0]))
    used = stacked[: turned.shape[1]]
    across = lax.dot_general(
        inverse, used, (((1,), (1,)), ((), ())), precision=HIGHEST, preferred_element_type=F32
    )
    basis[...] = across[:, :rows].T.astype(BF16)
    share = size // (2 * chips)
    me = lax.axis_index("pix")
    shape = (size // 2, size)
    to = lax.broadcasted_iota(jnp.int32, shape, 0)
    source = lax.broadcasted_iota(jnp.int32, shape, 1)
    chip = lax.rem(to // share + me // 2, chips)
    wanted = (2 * chip + lax.rem(me, 2)) * share + lax.rem(to, share)
    pick = jnp.where(wanted == source, 1.0, 0.0).astype(BF16)
    turned[...] = jnp.dot(pick, across.astype(BF16), preferred_element_type=F32).astype(BF16)
    for copy in copies:
        copy.wait()
    for n in range(2):
        put_parts(turned, held[n], factor, outs[n * chips : (n + 1) * chips])


def basis_of(sketches, ends, factor, chips, used):
    rows, size = sketches[0].shape
    edge = ends[0].shape[1]
    share = size // (2 * chips)
    return pl.pallas_call(
        functools.partial(basis_kernel, chips, factor, len(sketches)),
        in_specs=[VMEM] * len(sketches) + [ANY] * 4,
        out_specs=[VMEM] * (2 + 2 * chips),
        out_shape=[
            jax.ShapeDtypeStruct((rows, size), BF16),
            jax.ShapeDtypeStruct((size // 2, used * rows), BF16),
        ]
        + [jax.ShapeDtypeStruct((share, edge), BF16)] * (2 * chips),
        scratch_shapes=[
            pltpu.VMEM((2, 2 * rows, edge), BF16),
            pltpu.SemaphoreType.DMA((4,)),
        ],
        cost_estimate=COST,
        compiler_params=params(32),
    )(*sketches, *ends)


def put_parts(turned, cleaned, factor, outs):
    part = jnp.dot(turned[:, : cleaned.shape[0]], cleaned, preferred_element_type=F32) * factor
    share = outs[0].shape[0]
    for k, out in enumerate(outs):
        out[...] = part[k * share : (k + 1) * share].astype(BF16)


def project_kernel(count, factor, chips, turned, band, *refs):
    blocks, outs, done = refs[:6], refs[-1 - count * chips : -1], refs[-1]
    done[...] = jnp.zeros_like(done)
    cleaned = clean_all(blocks, band[...])
    for n in range(count):

        @pl.when(pl.program_id(0) == n)
        def _():
            put_parts(turned, cleaned, factor, outs[n * chips : (n + 1) * chips])


def clean_all(blocks, band):
    return jnp.concatenate(
        [
            clean(blocks[n + 1][...], blocks[n][...], blocks[n + 2][...], band)
            for n in range(0, len(blocks), 3)
        ],
        axis=0,
    )


def project(turned, band, spectra, near, start, size, count, factor, chips, wait):
    rows = spectra.shape[0]
    share = turned.shape[0] // chips
    return pl.pallas_call(
        functools.partial(project_kernel, count, factor, chips),
        grid=(count,),
        in_specs=[whole(turned.shape), whole(band.shape)]
        + inner_specs(rows, size, start) * 2
        + [ANY] * len(wait),
        out_specs=[whole((share, size))] * (count * chips) + [whole((8, TILE))],
        out_shape=[jax.ShapeDtypeStruct((share, size), BF16)] * (count * chips)
        + [jax.ShapeDtypeStruct((8, TILE), F32)],
        cost_estimate=COST,
        compiler_params=params(50),
    )(turned, band, spectra, spectra, spectra, near, near, near, *wait)


def project_whole_kernel(factor, turned, band, own, own_low, own_high, near, *refs):
    near_low, near_high, far, other = refs[:4]
    out, done = refs[-2], refs[-1]
    done[...] = jnp.zeros_like(done)
    taps = band[...]
    cleaned = [
        clean(own_low[...], own[...], own_high[...], taps),
        clean(near_low[...], near[...], near_high[...], taps),
    ]
    for one in (far, other):
        last = one.shape[1] - TILE
        cleaned.append(clean(one[:, :TILE], one[:, TILE:last], one[:, last:], taps))
    put_parts(turned.at[: out.shape[0]], jnp.concatenate(cleaned, axis=0), factor, [out])


def project_whole(out, turned, band, spectra, near, far, start, factor, wait):
    rows = spectra.shape[0]
    size = far[0].shape[1] - 2 * TILE
    return pl.pallas_call(
        functools.partial(project_whole_kernel, factor),
        grid=(1,),
        in_specs=[whole(turned.shape), whole(band.shape)]
        + inner_specs(rows, size, start) * 2
        + [whole(one.shape) for one in far]
        + [ANY] * (1 + len(wait)),
        out_specs=[at((out.shape[0], size), lambda i: start // TILE), whole((8, TILE))],
        out_shape=[
            jax.ShapeDtypeStruct(out.shape, BF16),
            jax.ShapeDtypeStruct((8, TILE), F32),
        ],
        input_output_aliases={10: 0},
        cost_estimate=COST,
        compiler_params=params(50),
    )(turned, band, *[spectra] * 3, *[near] * 3, *far, out, *wait)


def finish_kernel(blocks, count, *refs):
    out, done = refs[-2], refs[-1]
    done[...] = jnp.zeros_like(done)
    for n in range(blocks):

        @pl.when(pl.program_id(0) == n)
        def _():
            parts = refs[n * count : (n + 1) * count]
            out[...] = pairwise([part[...].astype(F32) for part in parts]).astype(BF16)


def finish(out, blocks, starts, bins, wait):
    parts = [part for block in blocks for part in block]
    share, size = parts[0].shape
    extra = [] if out is None else [out]
    return pl.pallas_call(
        functools.partial(finish_kernel, len(blocks), len(blocks[0])),
        grid=(len(blocks),),
        in_specs=[whole((share, size))] * len(parts) + [ANY] * (len(extra) + len(wait)),
        out_specs=[
            at(
                (share, size),
                lambda i: jnp.where(i == 0, starts[0] // TILE, starts[-1] // TILE),
            ),
            whole((8, TILE)),
        ],
        out_shape=[
            jax.ShapeDtypeStruct((share, bins), BF16),
            jax.ShapeDtypeStruct((8, TILE), F32),
        ],
        input_output_aliases={len(parts): 0} if extra else {},
        cost_estimate=COST,
        compiler_params=params(32),
    )(*parts, *extra, *wait)


def per_device(spectra, kernel, probes):
    rows, bins = spectra.shape
    pix = lax.axis_size("pix")
    depth = lax.axis_size("mz")
    chips = pix // 2
    factor = 1.0 / math.sqrt(float(rows * pix))

    def swap(first, tile):
        pairs = [(i, i + 1) for i in range(first, depth - 1, 2)]
        return lax.ppermute(tile, "mz", pairs + [(b, a) for a, b in pairs])

    lower = lax.rem(lax.axis_index("mz"), 2) == 0
    head, tail = spectra[:, :TILE], spectra[:, bins - TILE :]
    even = swap(0, jnp.where(lower, tail, head))
    odd = swap(1, jnp.where(lower, head, tail))
    taps = jnp.pad(kernel.astype(F32), (REACH, 2 * WIDTH - REACH - kernel.shape[0]))[None]

    near = partner(spectra, "pix", 1)
    edge = math.gcd(bins // 2, EDGE)
    far = []
    inner = edge
    if chips == 2 and bins >= 8 * EARLY:
        inner = edge + EARLY
        far = [partner(spectra[:, edge - TILE : inner + TILE], "pix", 2)]
    partial_sketch, band, first, final = sketch_of(taps, spectra, even, odd, probes, edge)
    ends = [first, partner(first, "pix", 1), final, partner(final, "pix", 1)]
    sketch = total_of(spread(partial_sketch, "mz"), far)
    basis, turned, *mine = basis_of(
        gather(sketch, "pix"), ends, factor, chips, 2 + 2 * len(far)
    )

    routes = [
        [
            (2 * chip + core, 2 * ((chip + k) % chips) + core)
            for chip in range(chips)
            for core in range(2)
        ]
        for k in range(chips)
    ]

    def across(mine):
        return [mine[0]] + [lax.ppermute(mine[m], "pix", routes[m]) for m in range(1, chips)]

    def across(mine):
        return [mine[0]] + [lax.ppermute(mine[m], "pix", routes[m]) for m in range(1, chips)]

    out, recent = None, []
    before = ([across(mine[:chips]), across(mine[chips:])], (0, bins - edge))
    start, stop = inner, bins - edge
    while start < stop:
        size = min(edge, stop - start)
        count = min(2, (stop - start) // size)
        *mine, done = project(
            turned, band, spectra, near, start, size, count, factor, chips, recent
        )
        blocks = [across(mine[n * chips : (n + 1) * chips]) for n in range(count)]
        recent = [done]
        places = tuple(start + n * size for n in range(count))
        start += count * size
        if far and start == stop:
            pair = [far[0], partner(far[0], "pix", 1)]
            out, done = project_whole(
                out, turned, band, spectra, near, pair, edge, factor, recent
            )
            recent = [done]
        out, done = finish(out, *before, bins, recent)
        recent = [done]
        before = (blocks, places)
    out, done = finish(out, *before, bins, recent)
    return (basis, out)


def solution(mesh):
    in_specs = (P(("groups", "pix"), "mz"), P(), P("mz", None))
    out_specs = (P(("groups", "pix"), None), P(("groups", "pix"), "mz"))
    return jax.shard_map(
        per_device, mesh=mesh, in_specs=in_specs, out_specs=out_specs, check_vma=False
    )
```

```python
import functools
import math

import jax
import jax.numpy as jnp
from jax import lax
from jax.experimental import pallas as pl
from jax.experimental.pallas import tpu as pltpu
from jax.sharding import PartitionSpec as P

F32 = jnp.float32
BF16 = jnp.bfloat16
HIGHEST = lax.Precision.HIGHEST
TILE = 128
WIDTH = 256
REACH = 64
EDGE = 4096
EARLY = 4096
VMEM = pl.BlockSpec(memory_space=pltpu.VMEM)


COST = pl.CostEstimate(flops=1, bytes_accessed=1, transcendentals=0)


def params(limit=56):
    return pltpu.CompilerParams(vmem_limit_bytes=limit * 2**20)


def partner(x, axis, shift):
    count = lax.axis_size(axis)
    return lax.ppermute(x, axis, [(i, i ^ shift) for i in range(count)])


def gather(x, axis):
    count = lax.axis_size(axis)
    if count & (count - 1):
        every = lax.all_gather(x, axis)
        return [every[k] for k in range(count)]
    return [x] + [partner(x, axis, shift) for shift in range(1, count)]


def spread(x, axis):
    count = lax.axis_size(axis)
    if count & (count - 1):
        return [lax.psum(x, axis)]
    shift = count // 2
    while shift >= 4:
        x = x + partner(x, axis, shift)
        shift //= 2
    if count >= 4:
        x = total_of([x, partner(x, axis, 1)], [])
    return [x, partner(x, axis, 2)]


def pairwise(parts):
    while len(parts) > 1:
        odd = [parts[-1]] if len(parts) % 2 else []
        parts = [a + b for a, b in zip(parts[::2], parts[1::2])] + odd
    return parts[0]


def band_of(taps):
    wide = jnp.broadcast_to(taps, (WIDTH, 2 * WIDTH))
    return pltpu.roll(wide, 0, 1, stride=1, stride_axis=0).T.astype(BF16)


def clean(before, block, after, band):
    ext = jnp.concatenate([before, block, after], axis=1)
    rows, bins = block.shape
    starts = range(0, bins, WIDTH)
    lhs = jnp.concatenate([ext[:, a : a + 2 * WIDTH] for a in starts], axis=0)
    base = jnp.dot(lhs, band, preferred_element_type=F32)
    mid = jnp.concatenate([block[:, a : a + WIDTH] for a in starts], axis=0)
    out = (mid.astype(F32) - base).astype(BF16)
    return jnp.concatenate([out[i * rows : (i + 1) * rows] for i in range(bins // WIDTH)], axis=1)


def sketch_kernel(steps, taps, even, odd, spectra, probes, *refs):
    sketch, band, first, final, ext, held, one, two, came, there = refs
    size = one.shape[1]
    bins = steps * size

    def bins_copy(c, last=False):
        skip = TILE if not isinstance(c, int) or c > 0 else 0
        width = size + TILE - skip - (TILE if last else 0)
        start = pl.multiple_of(c * size + skip, TILE)
        return pltpu.make_async_copy(
            spectra.at[:, pl.ds(start, width)], ext.at[:, pl.ds(start + TILE, width)], came.at[c]
        )

    def probes_copy(c):
        start = pl.multiple_of(c * size, size)
        return pltpu.make_async_copy(
            probes.at[pl.ds(start, size), :], held.at[pl.ds(start, size), :], there.at[c]
        )

    for c in range(steps):
        bins_copy(c, c == steps - 1).start()
        if c > 0:
            probes_copy(c - 1).start()
    probes_copy(steps - 1).start()
    lower = lax.rem(lax.axis_index("mz"), 2) == 0
    ext[:, :TILE] = jnp.where(lower, odd[...], even[...])
    ext[:, bins + TILE :] = jnp.where(lower, even[...], odd[...])
    band[...] = band_of(taps[...])
    sketch[...] = jnp.zeros_like(sketch)

    def filter_to(out, c):
        start = pl.multiple_of(c * size, size)

        def part(a, b):
            return ext[:, pl.ds(pl.multiple_of(start + a, TILE), b - a)]

        for a in range(0, size, WIDTH):
            base = jnp.dot(part(a, a + 2 * WIDTH), band[...], preferred_element_type=F32)
            block = part(a + TILE, a + TILE + WIDTH).astype(F32)
            out[:, a : a + WIDTH] = (block - base).astype(BF16)

    def add(cleaned, c):
        rows = held[pl.ds(pl.multiple_of(c * size, size), size), :]
        sketch[...] += jnp.dot(cleaned[...], rows, preferred_element_type=F32)

    bins_copy(0).wait()
    filter_to(one, 0)
    first[...] = one[:, : first.shape[1]]
    probes_copy(0).wait()

    def pair(k, carry):
        c = 2 * k + 1

        @pl.when(c + 1 < steps)
        def _():
            bins_copy(c).wait()

        @pl.when(c + 1 == steps)
        def _():
            bins_copy(c, True).wait()

        filter_to(two, c)
        add(one, c - 1)
        probes_copy(c).wait()

        @pl.when(c + 1 < steps)
        def _():
            bins_copy(c + 1).wait()
            filter_to(one, c + 1)
            add(two, c)
            probes_copy(c + 1).wait()

        return carry

    lax.fori_loop(0, steps // 2, pair, 0)
    add(two, steps - 1)
    final[...] = two[:, size - final.shape[1] :]


ANY = pl.BlockSpec(memory_space=pl.ANY)


def whole(shape):
    return pl.BlockSpec(shape, lambda i: (0, 0))


def at(shape, place):
    return pl.BlockSpec(
        tuple(pl.Element(n) for n in shape), lambda i: (0, place(i) * TILE)
    )


def inner_specs(rows, size, start):
    first, per = start // TILE, size // TILE
    return [
        at((rows, size), lambda i: first + i * per),
        at((rows, TILE), lambda i: first + i * per - 1),
        at((rows, TILE), lambda i: first + i * per + per),
    ]


def block_specs(rows, size, first, last):
    per = size // TILE
    return [
        pl.BlockSpec((rows, size), lambda i: (0, first + i)),
        pl.BlockSpec((rows, TILE), lambda i: (0, jnp.maximum((first + i) * per - 1, 0))),
        pl.BlockSpec((rows, TILE), lambda i: (0, jnp.minimum((first + i + 1) * per, last))),
    ]


def sketch_of(taps, spectra, even, odd, probes, edge):
    rows, bins = spectra.shape
    size = math.gcd(bins // 2, 8192)
    steps = bins // size
    columns = probes.shape[1]
    return pl.pallas_call(
        functools.partial(sketch_kernel, steps),
        in_specs=[VMEM] * 3 + [ANY] * 2,
        out_specs=[VMEM] * 4,
        out_shape=[
            jax.ShapeDtypeStruct((rows, columns), F32),
            jax.ShapeDtypeStruct((2 * WIDTH, WIDTH), BF16),
            jax.ShapeDtypeStruct((rows, edge), BF16),
            jax.ShapeDtypeStruct((rows, edge), BF16),
        ],
        scratch_shapes=[
            pltpu.VMEM((rows, bins + 2 * TILE), BF16),
            pltpu.VMEM((bins, columns), BF16),
            pltpu.VMEM((rows, size), BF16),
            pltpu.VMEM((rows, size), BF16),
            pltpu.SemaphoreType.DMA((steps,)),
            pltpu.SemaphoreType.DMA((steps,)),
        ],
        cost_estimate=COST,
        compiler_params=params(50),
    )(taps, even, odd, spectra, probes)


def total_kernel(count, *refs):
    refs[-1][...] = pairwise([part[...] for part in refs[:count]])


def total_of(parts, wait):
    return pl.pallas_call(
        functools.partial(total_kernel, len(parts)),
        in_specs=[VMEM] * len(parts) + [ANY] * len(wait),
        out_specs=VMEM,
        out_shape=jax.ShapeDtypeStruct(parts[0].shape, F32),
        cost_estimate=COST,
        compiler_params=params(32),
    )(*parts, *wait)


def inverse_factor(gram):
    size = gram.shape[0]
    groups = range(size // 8)
    rows = [gram[8 * g : 8 * g + 8] for g in groups]
    lane = lax.broadcasted_iota(jnp.int32, (8, size), 1)
    sub = lax.broadcasted_iota(jnp.int32, (8, size), 0)

    def row_of(x, k):
        return jnp.broadcast_to(x[k : k + 1], (8, size))

    result = []
    for g in groups:
        inside = (lane >= 8 * g) & (lane < 8 * g + 8)
        below = groups[g:]
        cols = {
            h: [
                jnp.broadcast_to(rows[h][:, 8 * g + k : 8 * g + k + 1], (8, size))
                for k in range(8)
            ]
            for h in below
        }
        for h in below:
            unit = jnp.where(lane - 8 * g == sub, 1.0, 0.0) if h == g else 0.0
            rows[h] = jnp.where(inside, unit, rows[h])
        pivots = jnp.ones((8, size), F32)
        for k in range(8):
            pivot = row_of(cols[g][k], k)
            scale = 1.0 / pivot
            pivots = jnp.where(sub == k, pivot, pivots)
            line = row_of(rows[g], k) * scale
            heads = {m: row_of(cols[g][m], k) * scale for m in range(k + 1, 8)}
            for h in below:
                c = cols[h][k]
                if h == g:
                    c = jnp.where(sub > k, c, 0.0)
                rows[h] = rows[h] - c * line
                for m in range(k + 1, 8):
                    cols[h][m] = cols[h][m] - c * heads[m]
        result.append(jnp.where(lane < 8 * g + 8, rows[g] * lax.rsqrt(pivots), 0.0))
    return jnp.concatenate(result, axis=0)


def basis_kernel(chips, factor, count, *refs):
    ends, (basis, turned) = refs[count : count + 4], refs[count + 4 : count + 6]
    outs, held, sems = refs[count + 6 : -2], refs[-2], refs[-1]
    rows = held.shape[1] // 2
    copies = [
        pltpu.make_async_copy(
            one, held.at[n // 2, pl.ds(n % 2 * rows, rows), :], sems.at[n]
        )
        for n, one in enumerate(ends)
    ]
    for copy in copies:
        copy.start()
    sketches = [ref[...] for ref in refs[:count]]
    size = sketches[0].shape[1]
    stacked = jnp.concatenate(sketches, axis=0)
    gram = lax.dot_general(
        stacked, stacked, (((0,), (0,)), ((), ())), precision=HIGHEST, preferred_element_type=F32
    )
    inverse = inverse_factor(gram / float(stacked.shape[0]))
    used = stacked[: turned.shape[1]]
    across = lax.dot_general(
        inverse, used, (((1,), (1,)), ((), ())), precision=HIGHEST, preferred_element_type=F32
    )
    basis[...] = across[:, :rows].T.astype(BF16)
    share = size // (2 * chips)
    me = lax.axis_index("pix")
    shape = (size // 2, size)
    to = lax.broadcasted_iota(jnp.int32, shape, 0)
    source = lax.broadcasted_iota(jnp.int32, shape, 1)
    chip = lax.rem(to // share + me // 2, chips)
    wanted = (2 * chip + lax.rem(me, 2)) * share + lax.rem(to, share)
    pick = jnp.where(wanted == source, 1.0, 0.0).astype(BF16)
    turned[...] = jnp.dot(pick, across.astype(BF16), preferred_element_type=F32).astype(BF16)
    for copy in copies:
        copy.wait()
    for n in range(2):
        put_parts(turned, held[n], factor, outs[n * chips : (n + 1) * chips])


def basis_of(sketches, ends, factor, chips, used):
    rows, size = sketches[0].shape
    edge = ends[0].shape[1]
    share = size // (2 * chips)
    return pl.pallas_call(
        functools.partial(basis_kernel, chips, factor, len(sketches)),
        in_specs=[VMEM] * len(sketches) + [ANY] * 4,
        out_specs=[VMEM] * (2 + 2 * chips),
        out_shape=[
            jax.ShapeDtypeStruct((rows, size), BF16),
            jax.ShapeDtypeStruct((size // 2, used * rows), BF16),
        ]
        + [jax.ShapeDtypeStruct((share, edge), BF16)] * (2 * chips),
        scratch_shapes=[
            pltpu.VMEM((2, 2 * rows, edge), BF16),
            pltpu.SemaphoreType.DMA((4,)),
        ],
        cost_estimate=COST,
        compiler_params=params(32),
    )(*sketches, *ends)


def put_parts(turned, cleaned, factor, outs):
    part = jnp.dot(turned[:, : cleaned.shape[0]], cleaned, preferred_element_type=F32) * factor
    share = outs[0].shape[0]
    for k, out in enumerate(outs):
        out[...] = part[k * share : (k + 1) * share].astype(BF16)


def project_kernel(count, factor, chips, turned, band, *refs):
    blocks, outs, done = refs[:6], refs[-1 - count * chips : -1], refs[-1]
    done[...] = jnp.zeros_like(done)
    cleaned = clean_all(blocks, band[...])
    for n in range(count):

        @pl.when(pl.program_id(0) == n)
        def _():
            put_parts(turned, cleaned, factor, outs[n * chips : (n + 1) * chips])


def clean_all(blocks, band):
    return jnp.concatenate(
        [
            clean(blocks[n + 1][...], blocks[n][...], blocks[n + 2][...], band)
            for n in range(0, len(blocks), 3)
        ],
        axis=0,
    )


def project(turned, band, spectra, near, start, size, count, factor, chips, wait):
    rows = spectra.shape[0]
    share = turned.shape[0] // chips
    return pl.pallas_call(
        functools.partial(project_kernel, count, factor, chips),
        grid=(count,),
        in_specs=[whole(turned.shape), whole(band.shape)]
        + inner_specs(rows, size, start) * 2
        + [ANY] * len(wait),
        out_specs=[whole((share, size))] * (count * chips) + [whole((8, TILE))],
        out_shape=[jax.ShapeDtypeStruct((share, size), BF16)] * (count * chips)
        + [jax.ShapeDtypeStruct((8, TILE), F32)],
        cost_estimate=COST,
        compiler_params=params(50),
    )(turned, band, spectra, spectra, spectra, near, near, near, *wait)


def project_whole_kernel(factor, turned, band, own, own_low, own_high, near, *refs):
    near_low, near_high, far, other = refs[:4]
    out, done = refs[-2], refs[-1]
    done[...] = jnp.zeros_like(done)
    taps = band[...]
    cleaned = [
        clean(own_low[...], own[...], own_high[...], taps),
        clean(near_low[...], near[...], near_high[...], taps),
    ]
    for one in (far, other):
        last = one.shape[1] - TILE
        cleaned.append(clean(one[:, :TILE], one[:, TILE:last], one[:, last:], taps))
    put_parts(turned.at[: out.shape[0]], jnp.concatenate(cleaned, axis=0), factor, [out])


def project_whole(out, turned, band, spectra, near, far, start, factor, wait):
    rows = spectra.shape[0]
    size = far[0].shape[1] - 2 * TILE
    return pl.pallas_call(
        functools.partial(project_whole_kernel, factor),
        grid=(1,),
        in_specs=[whole(turned.shape), whole(band.shape)]
        + inner_specs(rows, size, start) * 2
        + [whole(one.shape) for one in far]
        + [ANY] * (1 + len(wait)),
        out_specs=[at((out.shape[0], size), lambda i: start // TILE), whole((8, TILE))],
        out_shape=[
            jax.ShapeDtypeStruct(out.shape, BF16),
            jax.ShapeDtypeStruct((8, TILE), F32),
        ],
        input_output_aliases={10: 0},
        cost_estimate=COST,
        compiler_params=params(50),
    )(turned, band, *[spectra] * 3, *[near] * 3, *far, out, *wait)


def finish_kernel(blocks, count, *refs):
    out, done = refs[-2], refs[-1]
    done[...] = jnp.zeros_like(done)
    for n in range(blocks):

        @pl.when(pl.program_id(0) == n)
        def _():
            parts = refs[n * count : (n + 1) * count]
            out[...] = pairwise([part[...].astype(F32) for part in parts]).astype(BF16)


def finish(out, blocks, starts, bins, wait):
    parts = [part for block in blocks for part in block]
    share, size = parts[0].shape
    extra = [] if out is None else [out]
    return pl.pallas_call(
        functools.partial(finish_kernel, len(blocks), len(blocks[0])),
        grid=(len(blocks),),
        in_specs=[whole((share, size))] * len(parts) + [ANY] * (len(extra) + len(wait)),
        out_specs=[
            at(
                (share, size),
                lambda i: jnp.where(i == 0, starts[0] // TILE, starts[-1] // TILE),
            ),
            whole((8, TILE)),
        ],
        out_shape=[
            jax.ShapeDtypeStruct((share, bins), BF16),
            jax.ShapeDtypeStruct((8, TILE), F32),
        ],
        input_output_aliases={len(parts): 0} if extra else {},
        cost_estimate=COST,
        compiler_params=params(32),
    )(*parts, *extra, *wait)


def per_device(spectra, kernel, probes):
    rows, bins = spectra.shape
    pix = lax.axis_size("pix")
    depth = lax.axis_size("mz")
    chips = pix // 2
    factor = 1.0 / math.sqrt(float(rows * pix))

    def swap(first, tile):
        pairs = [(i, i + 1) for i in range(first, depth - 1, 2)]
        return lax.ppermute(tile, "mz", pairs + [(b, a) for a, b in pairs])

    lower = lax.rem(lax.axis_index("mz"), 2) == 0
    head, tail = spectra[:, :TILE], spectra[:, bins - TILE :]
    even = swap(0, jnp.where(lower, tail, head))
    odd = swap(1, jnp.where(lower, head, tail))
    taps = jnp.pad(kernel.astype(F32), (REACH, 2 * WIDTH - REACH - kernel.shape[0]))[None]

    near = partner(spectra, "pix", 1)
    edge = math.gcd(bins // 2, EDGE)
    far = []
    inner = edge
    if chips == 2 and bins >= 8 * EARLY:
        inner = edge + EARLY
        far = [partner(spectra[:, edge - TILE : inner + TILE], "pix", 2)]
    partial_sketch, band, first, final = sketch_of(taps, spectra, even, odd, probes, edge)
    ends = [first, partner(first, "pix", 1), final, partner(final, "pix", 1)]
    sketch = total_of(spread(partial_sketch, "mz"), far)
    basis, turned, *mine = basis_of(
        gather(sketch, "pix"), ends, factor, chips, 2 + 2 * len(far)
    )

    routes = [
        [
            (2 * chip + core, 2 * ((chip + k) % chips) + core)
            for chip in range(chips)
            for core in range(2)
        ]
        for k in range(chips)
    ]

    def across(mine):
        return [mine[0]] + [lax.ppermute(mine[m], "pix", routes[m]) for m in range(1, chips)]

    def across(mine):
        return [mine[0]] + [lax.ppermute(mine[m], "pix", routes[m]) for m in range(1, chips)]

    out, recent = None, []
    before = ([across(mine[:chips]), across(mine[chips:])], (0, bins - edge))
    start, stop = inner, bins - edge
    while start < stop:
        size = min(edge, stop - start)
        count = min(2, (stop - start) // size)
        *mine, done = project(
            turned, band, spectra, near, start, size, count, factor, chips, recent
        )
        blocks = [across(mine[n * chips : (n + 1) * chips]) for n in range(count)]
        recent = [done]
        places = tuple(start + n * size for n in range(count))
        start += count * size
        if far and start == stop:
            pair = [far[0], partner(far[0], "pix", 1)]
            out, done = project_whole(
                out, turned, band, spectra, near, pair, edge, factor, recent
            )
            recent = [done]
        out, done = finish(out, *before, bins, recent)
        recent = [done]
        before = (blocks, places)
    out, done = finish(out, *before, bins, recent)
    return (basis, out)


def solution(mesh):
    in_specs = (P(("groups", "pix"), "mz"), P(), P("mz", None))
    out_specs = (P(("groups", "pix"), None), P(("groups", "pix"), "mz"))
    return jax.shard_map(
        per_device, mesh=mesh, in_specs=in_specs, out_specs=out_specs, check_vma=False
    )
```
